32 devices in a mesh: layer: 8 (over y, x, core), dp: 4 (over z).
Axes of the slice: x: 2, y: 2, z: 4, core: 2. Of those that a mesh axis runs over, the one named last changes fastest.
Arguments:
- inputs: float32 [512, 1024], P('dp'), may hold values from -6 to 6
- guesses: float32 [8, 512, 1024], P('layer', 'dp'), may hold values from -6 to 6
- weights: bfloat16 [32, 1024, 1024], P('layer'), may hold values from -0.1875 to 0.1875
- biases: float32 [32, 1024], P('layer'), may hold values from -3 to 3
- adjoint: bfloat16 [8, 512, 1024], P('layer', 'dp'), may hold values from -6 to 6
Outputs:
- new_states: float32 [8, 512, 1024], P('layer', 'dp')
- coarse_states: float32 [8, 512, 1024], P('layer', 'dp')
- weight_grad: float32 [8, 1024, 1024], P('layer', None, 'dp')
The draws below stay inside these ranges and needn't reach their ends.
All inputs are finite; a program needn't handle non-finite values.
Results may differ from the reference program's by a relative error of at most 0.007.
Values may be sent and summed in bfloat16 or wider, within the bound.
No kernel may reach another device: no remote copies, remote signals or barrier semaphores. Data moves between devices by JAX's collectives and lax.ppermute only.
A program may use at most 64 MiB of HBM per device.

```python
import jax
import jax.numpy as jnp
from jax import lax

D = 1024
ROWS = 512
POINTS = 8
LAYERS = 32


def levels(key, shape, split, least, high):
    level, own = 1.0, jax.random.fold_in(key, 6)
    for axis_at, shards_of in split:
        draws = jnp.exp(jax.random.uniform(jax.random.fold_in(own, axis_at), (shards_of,), jnp.float32, least / len(split), high / len(split)))
        level = level * jnp.repeat(draws, shape[axis_at] // shards_of).reshape([-1 if axis == axis_at else 1 for axis in range(len(shape))])
    return level


def bell_draw(rng, dims, scale, limit, shards=(), held_as=jnp.bfloat16):
    factor_of = levels(rng, dims, shards, -0.22, 0.18) if shards else 1.0
    drawn = jax.random.normal(rng, dims, jnp.float32) * scale * factor_of
    return jnp.minimum(jnp.maximum(drawn, -limit), limit).astype(held_as)


def setup_inputs(seed: int = 0) -> dict:
    key_of = jax.random.split(jax.random.key(seed), 6)
    return {
        "inputs": bell_draw(key_of[0], (ROWS, D), 1.0, 6.0, ((0, 4),), jnp.float32),
        "guesses": bell_draw(key_of[1], (POINTS, ROWS, D), 1.0, 6.0, ((0, 8), (1, 4)), jnp.float32),
        "weights": bell_draw(key_of[2], (LAYERS, D, D), D ** -0.5, 0.1875, ((0, 8),)),
        "biases": bell_draw(key_of[3], (LAYERS, D), 0.5, 3.0, ((0, 8),), jnp.float32),
        "adjoint": bell_draw(key_of[4], (POINTS, ROWS, D), 1.0, 6.0, ((0, 8), (1, 4))),
    }


def matmul_all(states, weight_stack):
    return jnp.einsum('prd,pde->pre', states.astype(jnp.bfloat16).astype(jnp.float32), weight_stack.astype(jnp.float32))


def advance_all(states, weight_stack, bias_stack, step_size):
    pre_tanh = matmul_all(states, weight_stack) + bias_stack[:, None, :]
    return states + step_size * jnp.tanh(pre_tanh), pre_tanh


def previous(inputs, states):
    return jnp.concatenate([inputs[None], states[:-1]], axis=0)


def fine_all(starts, weights, biases, step_size):
    current = starts
    last_in = starts
    pre_tanh = starts
    for layer_idx in range(4):
        if layer_idx == 3:
            last_in = current
        current, pre_tanh = advance_all(current, weights[layer_idx::4], biases[layer_idx::4], step_size)
    return current, last_in, pre_tanh


def reference(inputs, guesses, weights, biases, adjoint):
    step_size = 4.0 / LAYERS
    coarse_w = weights[0::4]
    coarse_b = biases[0::4]
    groups = POINTS // 4
    relaxed = fine_all(previous(inputs, guesses), weights, biases, step_size)[0]
    relaxed_prev = previous(inputs, relaxed)
    ahead = fine_all(relaxed_prev, weights, biases, step_size)[0]
    forcing = ahead - advance_all(relaxed_prev, coarse_w, coarse_b, 4.0 * step_size)[0]
    group_w = coarse_w.reshape(groups, 4, D, D)
    group_b = coarse_b.reshape(groups, 4, D)
    group_f = forcing.reshape(groups, 4, ROWS, D)
    values = relaxed.reshape(groups, 4, ROWS, D)

    def level_step(states, slot):
        return advance_all(states, group_w[:, slot], group_b[:, slot], 4.0 * step_size)[0] + group_f[:, slot]

    def c_prev(values):
        return jnp.concatenate([inputs[None], values[:-1, 3]], axis=0)

    def f_relax(values):
        start = c_prev(values)
        for slot in range(3):
            start = level_step(start, slot)
            values = values.at[:, slot].set(start)
        return values

    values = f_relax(values)
    values = values.at[:, 3].set(level_step(values[:, 2], 3))
    values = f_relax(values)
    flat = values.reshape(POINTS, ROWS, D)
    update = advance_all(previous(inputs, flat), coarse_w, coarse_b, 4.0 * step_size)[0] + forcing
    start_block = jnp.broadcast_to(inputs[None], (4, ROWS, D))
    below = jnp.concatenate([start_block, flat[:-4]], axis=0)
    coarse_force = update - advance_all(below, coarse_w, coarse_b, 16.0 * step_size)[0]

    def chain_step(carry, pieces):
        weight, bias_row, force = pieces
        result = advance_all(carry, weight, bias_row, 16.0 * step_size)[0] + force
        return result, result

    _, solved = lax.scan(chain_step, start_block, (group_w, group_b, coarse_force.reshape(groups, 4, ROWS, D)))
    values = values.at[:, 3].set(solved[:, 3])
    coarse_states = solved.reshape(POINTS, ROWS, D) - relaxed
    values = f_relax(values)
    corrected = values.reshape(POINTS, ROWS, D)
    new_states, last_in, pre_tanh = fine_all(previous(inputs, corrected), weights, biases, step_size)
    tanh_val = jnp.tanh(pre_tanh)
    deltas = (adjoint.astype(jnp.float32) * step_size * (1.0 - tanh_val * tanh_val)).astype(jnp.bfloat16)
    weight_grad = jnp.einsum('prd,pre->pde', last_in.astype(jnp.bfloat16).astype(jnp.float32), deltas.astype(jnp.float32))
    return new_states, coarse_states, weight_grad
```

```python
import functools

import jax
import jax.numpy as jnp
from jax import lax
from jax.experimental import pallas as pl
from jax.experimental.pallas import tpu as pltpu
from jax.sharding import PartitionSpec as P

BF16 = jnp.bfloat16
F32 = jnp.float32
TILE = 256
EXTRA = 16
WHOLE = pl.BlockSpec(memory_space=pltpu.VMEM)
BULK = pl.BlockSpec(memory_space=pltpu.HBM)


def call(kernel, outs, *args, scratch=(), flops=0, specs=None):
    moved = sum(a.size * a.dtype.itemsize for a in args)
    return pl.pallas_call(
        kernel,
        out_shape=outs,
        in_specs=specs or [WHOLE] * len(args),
        out_specs=jax.tree.map(lambda _: WHOLE, outs, is_leaf=lambda leaf: not isinstance(leaf, (tuple, list))),
        scratch_shapes=list(scratch),
        compiler_params=pltpu.CompilerParams(vmem_limit_bytes=24 << 20),
        cost_estimate=pl.CostEstimate(flops=flops, bytes_accessed=moved, transcendentals=0),
    )(*args)


def kept(like, dtype=None):
    return pltpu.VMEM(like.shape, dtype or like.dtype)


def plain(shape, dtype):
    return jax.ShapeDtypeStruct(shape, dtype)


def tiles(width):
    step = min(TILE, width)
    return [slice(at, at + step) for at in range(0, width, step)]


def layer_of(rounded_ref, weight_ref, bias, cols):
    product = jnp.dot(rounded_ref[...], weight_ref[:, cols], preferred_element_type=F32)
    return jnp.tanh(product + bias[:, cols])


def load_kernel(source, target, coarse, sems):
    layers = source.shape[0]
    copies = [pltpu.make_async_copy(source.at[i], target.at[i], sems.at[i]) for i in range(layers)]
    copies.append(pltpu.make_async_copy(source.at[0], coarse, sems.at[layers]))
    for copy in copies:
        copy.start()
    for copy in copies:
        copy.wait()


def run_layers(layers, step_size, weights, biases, state, rounded):
    for layer in layers:
        bias = biases[layer : layer + 1, :]
        now, later = rounded[layer % 2], rounded[(layer + 1) % 2]
        for cols in tiles(state.shape[1]):
            new = state[:, cols] + step_size * layer_of(now, weights.at[layer], bias, cols)
            state[:, cols] = new
            later[:, cols] = new.astype(BF16)


def relax_kernel(step_size, rows, weights, biases, inputs, got, relaxed, sent, even, odd):
    first = lax.axis_index("layer") == 0

    @pl.when(first)
    def _():
        relaxed[...] = inputs[...]

    @pl.when(jnp.logical_not(first))
    def _():
        relaxed[...] = got[...].astype(F32)

    even[...] = relaxed[...].astype(BF16)
    run_layers(range(4), step_size, weights, biases, relaxed, (even, odd))
    sent[:rows, :] = even[...]
    bias = biases[0:1, :]
    high = bias.astype(BF16)
    rest = bias - high.astype(F32)
    middle = rest.astype(BF16)
    low = (rest - middle.astype(F32)).astype(BF16)
    at = lax.broadcasted_iota(jnp.int32, (EXTRA, bias.shape[1]), 0)
    parts = jnp.where(at == 0, high.astype(F32), jnp.where(at == 1, middle.astype(F32), low.astype(F32)))
    sent[rows:, :] = jnp.where(at < 3, parts, 0.0).astype(BF16)


def ahead_kernel(step_size, rows, weights, biases, inputs, got, start, forcing, pair_bias, top, sent_forcing, state, even, odd):
    first = lax.axis_index("layer") == 0

    @pl.when(first)
    def _():
        start[...] = inputs[...]

    @pl.when(jnp.logical_not(first))
    def _():
        start[...] = got[:rows, :].astype(F32)

    even[...] = start[...].astype(BF16)
    bias = biases[0:1, :]
    for cols in tiles(state.shape[1]):
        slope = layer_of(even, weights.at[0], bias, cols)
        new = start[:, cols] + step_size * slope
        state[:, cols] = new
        odd[:, cols] = new.astype(BF16)
        forcing[:, cols] = start[:, cols] + (4.0 * step_size) * slope
    run_layers((1, 2, 3), step_size, weights, biases, state, (even, odd))
    top[...] = even[...]
    difference = state[...] - forcing[...]
    forcing[...] = difference
    sent_forcing[...] = difference.astype(BF16)
    tail = got[rows:, :].astype(F32)
    pair_bias[...] = jnp.broadcast_to(tail[0:1, :] + (tail[1:2, :] + tail[2:3, :]), pair_bias.shape)


def coarse_kernel(chosen, factor, weights, biases, forcing, pair_weight, pair_bias, pair_forcing, got, mid, *rest):
    even, odd = rest[-2:]
    here = lax.axis_index("layer")

    @pl.when(chosen(here % 4, here // 4))
    def _():
        even[...] = got[...]
        for cols in tiles(mid.shape[1]):
            slope = layer_of(even, pair_weight, pair_bias[0:1, :], cols)
            new = got[:, cols].astype(F32) + factor * slope + pair_forcing[:, cols].astype(F32)
            mid[:, cols] = new
            odd[:, cols] = new.astype(BF16)
        bias = biases[0:1, :]
        for top in rest[:-2]:
            for cols in tiles(mid.shape[1]):
                slope = layer_of(odd, weights.at[0], bias, cols)
                top[:, cols] = (mid[:, cols] + factor * slope + forcing[:, cols]).astype(BF16)


def final_kernel(step_size, weights, biases, inputs, one, down, low_mid, first_mid, high_mid, forcing, relaxed, left, state, coarse, even, odd):
    here = lax.axis_index("layer")
    slot, group = here % 4, here // 4

    def start_from(condition, source):
        @pl.when(condition)
        def _():
            state[...] = source[...].astype(F32)

    start_from(here == 0, inputs)
    start_from(here == 1, one)
    start_from((here > 0) & (here % 2 == 0), down)
    start_from((slot == 1) & (group > 0), low_mid)
    start_from((slot == 3) & (group == 0), first_mid)
    start_from((slot == 3) & (group > 0), high_mid)
    even[...] = state[...].astype(BF16)
    bias = biases[0:1, :]
    for cols in tiles(state.shape[1]):
        slope = layer_of(even, weights.at[0], bias, cols)
        old = state[:, cols]
        new = old + step_size * slope
        coarse[:, cols] = old + (4.0 * step_size) * slope + forcing[:, cols] - relaxed[:, cols]
        state[:, cols] = new
        odd[:, cols] = new.astype(BF16)
    run_layers((1, 2), step_size, weights, biases, state, (even, odd))
    left[...] = odd[...]


def last_kernel(step_size, weights, biases, left, state, new_states):
    bias = biases[3:4, :]
    for cols in tiles(state.shape[1]):
        new_states[:, cols] = state[:, cols] + step_size * layer_of(left, weights.at[3], bias, cols)


def grad_kernel(step_size, count, has_total, weights, biases, *refs):
    lefts, adjoints = refs[:count], refs[count : 2 * count]
    total, deltas = refs[-2], refs[-1]
    width = total.shape[1]
    cols = pl.ds(pl.multiple_of(lax.axis_index("dp") * width, width), width)
    weight, bias = weights[3, :, cols], biases[3:4, cols]
    result = refs[2 * count][...] if has_total else None
    for rows, adjoint in zip(lefts, adjoints):
        slope = jnp.tanh(jnp.dot(rows[...], weight, preferred_element_type=F32) + bias)
        deltas[...] = (adjoint[...].astype(F32) * step_size * (1.0 - slope * slope)).astype(BF16)
        part = lax.dot_general(rows[...], deltas[...], (((0,), (0,)), ((), ())), preferred_element_type=F32)
        result = part if result is None else result + part
    total[...] = result


def single_kernel(factor, weights, biases, got, added, out):
    for cols in tiles(out.shape[1]):
        slope = layer_of(got, weights.at[0], biases[0:1, :], cols)
        out[:, cols] = got[:, cols].astype(F32) + factor * slope + added[:, cols]


def pick_kernel(chosen, new, old, out):
    here = lax.axis_index("layer")
    out[...] = jnp.where(chosen(here % 4, here // 4), new[...], old[...])


def body(inputs, guesses, weights, biases, adjoint):
    blocks = lax.axis_size("layer")
    parts = lax.axis_size("dp")
    groups = blocks // 4
    step_size = 4.0 / (4 * blocks)
    part = lax.axis_index("dp")
    rows, depth = inputs.shape
    width = depth // parts
    layer_flops = 2 * rows * depth * depth

    def along(state, pairs):
        return lax.ppermute(state, "layer", pairs)

    def shifted(array, by):
        return lax.ppermute(array, "dp", [(i, (i + by) % parts) for i in range(parts)])

    def adjoint_for(index):
        return lax.dynamic_slice_in_dim(adjoint[0], index * width, width, axis=1)

    up = [(i, i + 1) for i in range(blocks - 1)]
    up_pair = [(i, i + 1) for i in range(0, blocks, 2)]
    down_pair = [(i + 1, i) for i in range(0, blocks, 2)]
    rounded = [pltpu.VMEM((rows, depth), BF16)] * 2

    guess_sent, weights = lax.optimization_barrier((guesses[0].astype(BF16), weights))
    guess_prev = along(guess_sent, up)
    held_weights, coarse_weight = call(
        load_kernel,
        (kept(weights), plain(weights.shape[1:], BF16)),
        pltpu.with_memory_space_constraint(weights, pltpu.HBM),
        scratch=[pltpu.SemaphoreType.DMA((weights.shape[0] + 1,))], specs=[BULK],
    )
    relaxed, relaxed_sent = call(
        functools.partial(relax_kernel, step_size, rows),
        (kept(inputs), plain((rows + EXTRA, depth), BF16)),
        held_weights, biases, inputs, guess_prev,
        scratch=rounded, flops=4 * layer_flops,
    )
    pair_weight = along(coarse_weight, up_pair)
    sent_adjoints = [adjoint_for((part + by) % parts) for by in range(parts)]
    relaxed_sent, *sent_adjoints = lax.optimization_barrier((relaxed_sent, *sent_adjoints))
    relaxed_got = along(relaxed_sent, up)
    adjoints = sent_adjoints[:1] + [shifted(sent_adjoints[by], by) for by in range(1, parts)]
    relaxed_got, *adjoints = lax.optimization_barrier((relaxed_got, *adjoints))
    start, forcing, pair_bias, ahead, forcing_sent = call(
        functools.partial(ahead_kernel, step_size, rows),
        (kept(inputs), kept(inputs), pltpu.VMEM((8, depth), F32), plain((rows, depth), BF16), plain((rows, depth), BF16)),
        held_weights, biases, inputs, relaxed_got,
        scratch=[pltpu.VMEM((rows, depth), F32)] + rounded, flops=4 * layer_flops,
    )
    pair_forcing = along(forcing_sent, up_pair)

    def two_steps(top, pairs, chosen, last=False):
        got = along(top, pairs)
        mid, *new_top = call(
            functools.partial(coarse_kernel, chosen, 4.0 * step_size),
            (kept(inputs),) if last else (kept(inputs), plain((rows, depth), BF16)),
            held_weights, biases, forcing, pair_weight, pair_bias, pair_forcing, got,
            scratch=rounded, flops=2 * layer_flops,
        )
        return got, mid, *new_top

    here = lax.axis_index("layer")
    slot, group = here % 4, here // 4
    last_group = groups - 1

    def single(factor, got, added):
        return call(
            functools.partial(single_kernel, factor), plain((rows, depth), F32),
            held_weights, biases, got, added, flops=layer_flops,
        )

    def finish(gots, mids):
        got_1, got_2, got_3 = gots
        mid_1, mid_2, mid_3 = mids
        held = jnp.where(slot == 1, got_2, jnp.where(group == 0, got_1, got_3))
        down = along(held, down_pair)
        return call(
            functools.partial(final_kernel, step_size),
            (plain((rows, depth), BF16), kept(inputs), plain((rows, depth), F32)),
            held_weights, biases, inputs, start, down, mid_2, mid_1, mid_3, forcing, relaxed,
            scratch=rounded, flops=3 * layer_flops,
        )

    top_0 = ahead
    if groups > 2:
        after = single(4.0 * step_size, along(ahead, up_pair), forcing)
        top_0 = jnp.where((slot == 1) & (group > 0), after.astype(BF16), ahead)
    got_1, mid_1, top_1 = two_steps(
        top_0, [(4 * m + 1, 4 * m + 3) for m in range(groups - 1)], lambda slot, group: (slot == 3) & (group < last_group)
    )
    got_2, mid_2, top_2 = two_steps(
        top_1, [(4 * m - 1, 4 * m + 1) for m in range(1, groups)], lambda slot, group: (slot == 1) & (group > 0)
    )
    got_3, mid_3 = two_steps(
        top_2, [(4 * m + 1, 4 * m + 3) for m in range(1, groups)], lambda slot, group: (slot == 3) & (group > 0), True
    )
    left, state, coarse_states = finish((got_1, got_2, got_3), (mid_1, mid_2, mid_3))
    if groups > 2:
        late = lambda slot, group: group > 1
        relaxed_out = call(functools.partial(pick_kernel, late), plain((rows, depth), F32), relaxed, relaxed)
        solved = coarse_states + relaxed_out
        below = along(top_1, [(4 * m - 1, 4 * m + 3) for m in range(2, groups)])
        base = solved - single(16.0 * step_size, below, jnp.zeros((rows, depth), F32))
        for m in range(2, groups):
            new = single(16.0 * step_size, along(solved.astype(BF16), [(4 * m - 1, 4 * m + 3)]), base)
            solved = jnp.where(here == 4 * m + 3, new, solved)
        new_2, new_mid_2, top_2 = two_steps(
            solved.astype(BF16), [(4 * m - 1, 4 * m + 1) for m in range(2, groups)], lambda slot, group: (slot == 1) & (group > 1)
        )
        new_3, new_mid_3 = two_steps(
            top_2, [(4 * m + 1, 4 * m + 3) for m in range(2, groups)], lambda slot, group: (slot == 3) & (group > 1), True
        )
        mids = [
            call(functools.partial(pick_kernel, late), kept(inputs), new, old)
            for new, old in ((new_mid_2, mid_2), (new_mid_3, mid_3))
        ]
        gots = [jnp.where(group > 1, new, old) for new, old in ((new_2, got_2), (new_3, got_3))]
        left, state, coarse_early = finish((got_1, *gots), (mid_1, *mids))
        coarse_states = jnp.where(slot == 3, solved - relaxed_out, coarse_states)
    lefts = [left] + [shifted(left, by) for by in range(1, parts)]
    new_states = call(
        functools.partial(last_kernel, step_size), plain((rows, depth), F32),
        held_weights, biases, left, state, flops=layer_flops,
    )
    half = parts // 2
    deltas = [pltpu.VMEM((rows, width), BF16)]
    total = call(
        functools.partial(grad_kernel, step_size, half, False), pltpu.VMEM((depth, width), F32),
        held_weights, biases, *lefts[:half], *adjoints[:half], scratch=deltas, flops=layer_flops,
    )
    weight_grad = call(
        functools.partial(grad_kernel, step_size, parts - half, True), plain((depth, width), F32),
        held_weights, biases, *lefts[half:], *adjoints[half:], total, scratch=deltas, flops=layer_flops,
    )
    return (new_states[None], coarse_states[None], weight_grad[None])


def solution(mesh):
    return jax.shard_map(
        body,
        mesh=mesh,
        in_specs=(
            P("dp", None),
            P("layer", "dp", None),
            P("layer", None, None),
            P("layer", None),
            P("layer", "dp", None),
        ),
        out_specs=(P("layer", "dp", None), P("layer", "dp", None), P("layer", None, "dp")),
        check_vma=False,
    )
```

```python
import functools

import jax
import jax.numpy as jnp
from jax import lax
from jax.experimental import pallas as pl
from jax.experimental.pallas import tpu as pltpu
from jax.sharding import PartitionSpec as P

BF16 = jnp.bfloat16
F32 = jnp.float32
TILE = 256
EXTRA = 16
WHOLE = pl.BlockSpec(memory_space=pltpu.VMEM)
BULK = pl.BlockSpec(memory_space=pltpu.HBM)


def call(kernel, outs, *args, scratch=(), flops=0, specs=None):
    moved = sum(a.size * a.dtype.itemsize for a in args)
    return pl.pallas_call(
        kernel,
        out_shape=outs,
        in_specs=specs or [WHOLE] * len(args),
        out_specs=jax.tree.map(lambda _: WHOLE, outs, is_leaf=lambda leaf: not isinstance(leaf, (tuple, list))),
        scratch_shapes=list(scratch),
        compiler_params=pltpu.CompilerParams(vmem_limit_bytes=8 << 20),
        cost_estimate=pl.CostEstimate(flops=flops, bytes_accessed=moved, transcendentals=0),
    )(*args)


def kept(like, dtype=None):
    return pltpu.VMEM(like.shape, dtype or like.dtype)


def plain(shape, dtype):
    return jax.ShapeDtypeStruct(shape, dtype)


def tiles(width):
    step = min(TILE, width)
    return [slice(at, at + step) for at in range(0, width, step)]


def layer_of(rounded_ref, weight_ref, bias, cols):
    product = jnp.dot(rounded_ref[...], weight_ref[:, cols], preferred_element_type=F32)
    return jnp.tanh(product + bias[:, cols])


def prepare_kernel(parts, guess, adjoint, sent_guess, *columns):
    sent_guess[...] = guess[...].astype(BF16)
    width = adjoint.shape[1] // parts
    for by, target in enumerate(columns):
        index = lax.rem(lax.axis_index("dp") + by, parts)
        target[...] = adjoint[:, pl.ds(pl.multiple_of(index * width, width), width)]


def load_kernel(source, target, sems):
    layers, depth = source.shape[:2]
    pieces = sems.shape[0] // layers
    step = depth // pieces
    copies = [
        pltpu.make_async_copy(
            source.at[i, pl.ds(at * step, step)], target.at[i, pl.ds(at * step, step)], sems.at[i * pieces + at]
        )
        for i in range(layers)
        for at in range(pieces)
    ]
    for copy in copies:
        copy.start()
    for copy in copies:
        copy.wait()


def coarse_weight_kernel(weights, after, coarse_weight, sem):
    copy = pltpu.make_async_copy(weights.at[0], coarse_weight, sem)
    copy.start()
    copy.wait()


def run_layers(layers, step_size, weights, biases, state, rounded):
    for layer in layers:
        bias = biases[layer : layer + 1, :]
        now, later = rounded[layer % 2], rounded[(layer + 1) % 2]
        for cols in tiles(state.shape[1]):
            new = state[:, cols] + step_size * layer_of(now, weights.at[layer], bias, cols)
            state[:, cols] = new
            later[:, cols] = new.astype(BF16)


def relax_kernel(step_size, rows, weights, biases, inputs, got, relaxed, sent, even, odd):
    first = lax.axis_index("layer") == 0

    @pl.when(first)
    def _():
        relaxed[...] = inputs[...]

    @pl.when(jnp.logical_not(first))
    def _():
        relaxed[...] = got[...].astype(F32)

    even[...] = relaxed[...].astype(BF16)
    run_layers(range(4), step_size, weights, biases, relaxed, (even, odd))
    sent[:rows, :] = even[...]
    bias = biases[0:1, :]
    high = bias.astype(BF16)
    rest = bias - high.astype(F32)
    middle = rest.astype(BF16)
    low = (rest - middle.astype(F32)).astype(BF16)
    at = lax.broadcasted_iota(jnp.int32, (EXTRA, bias.shape[1]), 0)
    parts = jnp.where(at == 0, high.astype(F32), jnp.where(at == 1, middle.astype(F32), low.astype(F32)))
    sent[rows:, :] = jnp.where(at < 3, parts, 0.0).astype(BF16)


def ahead_kernel(step_size, rows, weights, biases, inputs, got, start, forcing, pair_bias, top, sent_forcing, state, even, odd):
    first = lax.axis_index("layer") == 0

    @pl.when(first)
    def _():
        start[...] = inputs[...]

    @pl.when(jnp.logical_not(first))
    def _():
        start[...] = got[:rows, :].astype(F32)

    even[...] = start[...].astype(BF16)
    bias = biases[0:1, :]
    for cols in tiles(state.shape[1]):
        slope = layer_of(even, weights.at[0], bias, cols)
        new = start[:, cols] + step_size * slope
        state[:, cols] = new
        odd[:, cols] = new.astype(BF16)
        forcing[:, cols] = start[:, cols] + (4.0 * step_size) * slope
    run_layers((1, 2, 3), step_size, weights, biases, state, (even, odd))
    top[...] = even[...]
    difference = state[...] - forcing[...]
    forcing[...] = difference
    sent_forcing[...] = difference.astype(BF16)
    tail = got[rows:, :].astype(F32)
    pair_bias[...] = jnp.broadcast_to(tail[0:1, :] + (tail[1:2, :] + tail[2:3, :]), pair_bias.shape)


def coarse_kernel(chosen, factor, weights, biases, forcing, pair_weight, pair_bias, pair_forcing, got, mid, *rest):
    even, odd = rest[-2:]
    here = lax.axis_index("layer")

    @pl.when(chosen(here % 4, here // 4))
    def _():
        even[...] = got[...]
        for cols in tiles(mid.shape[1]):
            slope = layer_of(even, pair_weight, pair_bias[0:1, :], cols)
            new = got[:, cols].astype(F32) + factor * slope + pair_forcing[:, cols].astype(F32)
            mid[:, cols] = new
            odd[:, cols] = new.astype(BF16)
        bias = biases[0:1, :]
        for top in rest[:-2]:
            for cols in tiles(mid.shape[1]):
                slope = layer_of(odd, weights.at[0], bias, cols)
                top[:, cols] = (mid[:, cols] + factor * slope + forcing[:, cols]).astype(BF16)


def held_kernel(got_1, got_2, got_3, held):
    here = lax.axis_index("layer")
    low, early = here % 4 < 2, here // 4 == 0
    held[...] = jnp.where(low, got_2[...], jnp.where(early, got_1[...], got_3[...]))


def final_kernel(step_size, weights, biases, inputs, one, down, low_mid, first_mid, high_mid, forcing, relaxed, left, state, coarse, even, odd):
    here = lax.axis_index("layer")
    slot, group = here % 4, here // 4

    def start_from(condition, source):
        @pl.when(condition)
        def _():
            state[...] = source[...].astype(F32)

    start_from(here == 0, inputs)
    start_from(here == 1, one)
    start_from((here > 0) & (here % 2 == 0), down)
    start_from((slot == 1) & (group > 0), low_mid)
    start_from((slot == 3) & (group == 0), first_mid)
    start_from((slot == 3) & (group > 0), high_mid)
    even[...] = state[...].astype(BF16)
    bias = biases[0:1, :]
    for cols in tiles(state.shape[1]):
        slope = layer_of(even, weights.at[0], bias, cols)
        old = state[:, cols]
        new = old + step_size * slope
        coarse[:, cols] = old + (4.0 * step_size) * slope + forcing[:, cols] - relaxed[:, cols]
        state[:, cols] = new
        odd[:, cols] = new.astype(BF16)
    run_layers((1, 2), step_size, weights, biases, state, (even, odd))
    left[...] = odd[...]


def last_kernel(step_size, weights, biases, left, state, new_states):
    bias = biases[3:4, :]
    for cols in tiles(state.shape[1]):
        new_states[:, cols] = state[:, cols] + step_size * layer_of(left, weights.at[3], bias, cols)


def grad_kernel(step_size, count, has_total, weights, biases, *refs):
    lefts, adjoints = refs[:count], refs[count : 2 * count]
    total, deltas = refs[-2], refs[-1]
    width = total.shape[1]
    cols = pl.ds(pl.multiple_of(lax.axis_index("dp") * width, width), width)
    weight, bias = weights[3, :, cols], biases[3:4, cols]
    result = refs[2 * count][...] if has_total else None
    for rows, adjoint in zip(lefts, adjoints):
        slope = jnp.tanh(jnp.dot(rows[...], weight, preferred_element_type=F32) + bias)
        deltas[...] = (adjoint[...].astype(F32) * step_size * (1.0 - slope * slope)).astype(BF16)
        part = lax.dot_general(rows[...], deltas[...], (((0,), (0,)), ((), ())), preferred_element_type=F32)
        result = part if result is None else result + part
    total[...] = result


def single_kernel(factor, weights, biases, got, added, out):
    for cols in tiles(out.shape[1]):
        slope = layer_of(got, weights.at[0], biases[0:1, :], cols)
        out[:, cols] = got[:, cols].astype(F32) + factor * slope + added[:, cols]


def pick_kernel(chosen, new, old, out):
    here = lax.axis_index("layer")
    out[...] = jnp.where(chosen(here % 4, here // 4), new[...], old[...])


def body(inputs, guesses, weights, biases, adjoint):
    blocks = lax.axis_size("layer")
    parts = lax.axis_size("dp")
    groups = blocks // 4
    step_size = 4.0 / (4 * blocks)
    rows, depth = inputs.shape
    width = depth // parts
    layer_flops = 2 * rows * depth * depth

    def along(state, pairs):
        return lax.ppermute(state, "layer", pairs)

    def shifted(array, by):
        return lax.ppermute(array, "dp", [(i, (i + by) % parts) for i in range(parts)])

    up = [(i, i + 1) for i in range(blocks - 1)]
    up_pair = [(i, i + 1) for i in range(0, blocks, 2)]
    down_pair = [(i + 1, i) for i in range(0, blocks, 2)]
    rounded = [pltpu.VMEM((rows, depth), BF16)] * 2

    guess_sent, *sent_adjoints = call(
        functools.partial(prepare_kernel, parts),
        (plain((rows, depth), BF16),) + (plain((rows, width), BF16),) * parts,
        guesses[0], adjoint[0],
    )
    guess_prev = along(guess_sent, up)
    guess_sent, weights = lax.optimization_barrier((guess_sent, weights))
    held_weights = call(
        load_kernel, kept(weights), pltpu.with_memory_space_constraint(weights, pltpu.HBM),
        scratch=[pltpu.SemaphoreType.DMA((weights.shape[0] * 4,))], specs=[BULK],
    )
    relaxed, relaxed_sent = call(
        functools.partial(relax_kernel, step_size, rows),
        (kept(inputs), plain((rows + EXTRA, depth), BF16)),
        held_weights, biases, inputs, guess_prev,
        scratch=rounded, flops=4 * layer_flops,
    )
    relaxed_got = along(relaxed_sent, up)
    coarse_weight = call(
        coarse_weight_kernel, plain((depth, depth), BF16), held_weights, relaxed_sent, scratch=[pltpu.SemaphoreType.DMA]
    )
    pair_weight = along(coarse_weight, up_pair)
    relaxed_got, pair_weight = lax.optimization_barrier((relaxed_got, pair_weight))
    start, forcing, pair_bias, ahead, forcing_sent = call(
        functools.partial(ahead_kernel, step_size, rows),
        (kept(inputs), kept(inputs), pltpu.VMEM((8, depth), F32), plain((rows, depth), BF16), plain((rows, depth), BF16)),
        held_weights, biases, inputs, relaxed_got,
        scratch=[pltpu.VMEM((rows, depth), F32)] + rounded, flops=4 * layer_flops,
    )
    pair_forcing = along(forcing_sent, up_pair)

    def two_steps(top, pairs, chosen, last=False, beside=()):
        got, *_ = lax.optimization_barrier((along(top, pairs), *beside))
        mid, *new_top = call(
            functools.partial(coarse_kernel, chosen, 4.0 * step_size),
            (kept(inputs),) if last else (kept(inputs), plain((rows, depth), BF16)),
            held_weights, biases, forcing, pair_weight, pair_bias, pair_forcing, got,
            scratch=rounded, flops=2 * layer_flops,
        )
        return got, mid, *new_top

    here = lax.axis_index("layer")
    slot, group = here % 4, here // 4
    last_group = groups - 1

    def single(factor, got, added):
        return call(
            functools.partial(single_kernel, factor), plain((rows, depth), F32),
            held_weights, biases, got, added, flops=layer_flops,
        )

    def finish(gots, mids):
        got_1, got_2, got_3 = gots
        mid_1, mid_2, mid_3 = mids
        held = call(held_kernel, plain((rows, depth), BF16), got_1, got_2, got_3)
        down = along(held, down_pair)
        return call(
            functools.partial(final_kernel, step_size),
            (plain((rows, depth), BF16), kept(inputs), plain((rows, depth), F32)),
            held_weights, biases, inputs, start, down, mid_2, mid_1, mid_3, forcing, relaxed,
            scratch=rounded, flops=3 * layer_flops,
        )

    top_0 = ahead
    if groups > 2:
        after = single(4.0 * step_size, along(ahead, up_pair), forcing)
        top_0 = jnp.where((slot == 1) & (group > 0), after.astype(BF16), ahead)
    got_1, mid_1, top_1 = two_steps(
        top_0, [(4 * m + 1, 4 * m + 3) for m in range(groups - 1)], lambda slot, group: (slot == 3) & (group < last_group)
    )
    top_1, *sent_adjoints = lax.optimization_barrier((top_1, *sent_adjoints))
    adjoints = sent_adjoints[:1] + [shifted(sent_adjoints[by], by) for by in range(1, parts)]
    got_2, mid_2, top_2 = two_steps(
        top_1, [(4 * m - 1, 4 * m + 1) for m in range(1, groups)], lambda slot, group: (slot == 1) & (group > 0),
        beside=adjoints,
    )
    got_3, mid_3 = two_steps(
        top_2, [(4 * m + 1, 4 * m + 3) for m in range(1, groups)], lambda slot, group: (slot == 3) & (group > 0), True
    )
    left, state, coarse_states = finish((got_1, got_2, got_3), (mid_1, mid_2, mid_3))
    if groups > 2:
        late = lambda slot, group: group > 1
        relaxed_out = call(functools.partial(pick_kernel, late), plain((rows, depth), F32), relaxed, relaxed)
        solved = coarse_states + relaxed_out
        below = along(top_1, [(4 * m - 1, 4 * m + 3) for m in range(2, groups)])
        base = solved - single(16.0 * step_size, below, jnp.zeros((rows, depth), F32))
        for m in range(2, groups):
            new = single(16.0 * step_size, along(solved.astype(BF16), [(4 * m - 1, 4 * m + 3)]), base)
            solved = jnp.where(here == 4 * m + 3, new, solved)
        new_2, new_mid_2, top_2 = two_steps(
            solved.astype(BF16), [(4 * m - 1, 4 * m + 1) for m in range(2, groups)], lambda slot, group: (slot == 1) & (group > 1)
        )
        new_3, new_mid_3 = two_steps(
            top_2, [(4 * m + 1, 4 * m + 3) for m in range(2, groups)], lambda slot, group: (slot == 3) & (group > 1), True
        )
        mids = [
            call(functools.partial(pick_kernel, late), kept(inputs), new, old)
            for new, old in ((new_mid_2, mid_2), (new_mid_3, mid_3))
        ]
        gots = [jnp.where(group > 1, new, old) for new, old in ((new_2, got_2), (new_3, got_3))]
        left, state, coarse_early = finish((got_1, *gots), (mid_1, *mids))
        coarse_states = jnp.where(slot == 3, solved - relaxed_out, coarse_states)
    lefts = [left] + [shifted(left, by) for by in range(1, parts)]
    new_states = call(
        functools.partial(last_kernel, step_size), plain((rows, depth), F32),
        held_weights, biases, left, state, flops=layer_flops,
    )
    half = parts // 2
    deltas = [pltpu.VMEM((rows, width), BF16)]
    total = call(
        functools.partial(grad_kernel, step_size, half, False), pltpu.VMEM((depth, width), F32),
        held_weights, biases, *lefts[:half], *adjoints[:half], scratch=deltas, flops=layer_flops,
    )
    weight_grad = call(
        functools.partial(grad_kernel, step_size, parts - half, True), plain((depth, width), F32),
        held_weights, biases, *lefts[half:], *adjoints[half:], total, scratch=deltas, flops=layer_flops,
    )
    return (new_states[None], coarse_states[None], weight_grad[None])


def solution(mesh):
    return jax.shard_map(
        body,
        mesh=mesh,
        in_specs=(
            P("dp", None),
            P("layer", "dp", None),
            P("layer", None, None),
            P("layer", None),
            P("layer", "dp", None),
        ),
        out_specs=(P("layer", "dp", None), P("layer", "dp", None), P("layer", None, "dp")),
        check_vma=False,
    )
```

```python
import functools

import jax
import jax.numpy as jnp
from jax import lax
from jax.experimental import pallas as pl
from jax.experimental.pallas import tpu as pltpu
from jax.sharding import PartitionSpec as P

BF16 = jnp.bfloat16
F32 = jnp.float32
TILE = 256
EXTRA = 16
WHOLE = pl.BlockSpec(memory_space=pltpu.VMEM)
BULK = pl.BlockSpec(memory_space=pltpu.HBM)


def call(kernel, outs, *args, scratch=(), flops=0, specs=None):
    moved = sum(a.size * a.dtype.itemsize for a in args)
    return pl.pallas_call(
        kernel,
        out_shape=outs,
        in_specs=specs or [WHOLE] * len(args),
        out_specs=jax.tree.map(lambda _: WHOLE, outs, is_leaf=lambda leaf: not isinstance(leaf, (tuple, list))),
        scratch_shapes=list(scratch),
        compiler_params=pltpu.CompilerParams(vmem_limit_bytes=8 << 20),
        cost_estimate=pl.CostEstimate(flops=flops, bytes_accessed=moved, transcendentals=0),
    )(*args)


def kept(like, dtype=None):
    return pltpu.VMEM(like.shape, dtype or like.dtype)


def plain(shape, dtype):
    return jax.ShapeDtypeStruct(shape, dtype)


def tiles(width):
    step = min(TILE, width)
    return [slice(at, at + step) for at in range(0, width, step)]


def layer_of(rounded_ref, weight_ref, bias, cols):
    product = jnp.dot(rounded_ref[...], weight_ref[:, cols], preferred_element_type=F32)
    return jnp.tanh(product + bias[:, cols])


def round_kernel(guess, sent_guess):
    sent_guess[...] = guess[...].astype(BF16)


def columns_kernel(parts, adjoint, *columns):
    width = adjoint.shape[1] // parts
    for by, target in enumerate(columns):
        index = lax.rem(lax.axis_index("dp") + by, parts)
        target[...] = adjoint[:, pl.ds(pl.multiple_of(index * width, width), width)]


def load_kernel(source, target, coarse_weight, sems):
    layers, depth = source.shape[:2]
    pieces = (sems.shape[0] - 1) // layers
    step = depth // pieces
    copies = [
        pltpu.make_async_copy(
            source.at[i, pl.ds(at * step, step)], target.at[i, pl.ds(at * step, step)], sems.at[i * pieces + at]
        )
        for i in range(layers)
        for at in range(pieces)
    ]
    for copy in copies:
        copy.start()
    for copy in copies[:pieces]:
        copy.wait()
    again = pltpu.make_async_copy(target.at[0], coarse_weight, sems.at[layers * pieces])
    again.start()
    for copy in copies[pieces:]:
        copy.wait()
    again.wait()


def run_layers(layers, step_size, weights, biases, state, rounded):
    for layer in layers:
        bias = biases[layer : layer + 1, :]
        now, later = rounded[layer % 2], rounded[(layer + 1) % 2]
        for cols in tiles(state.shape[1]):
            new = state[:, cols] + step_size * layer_of(now, weights.at[layer], bias, cols)
            state[:, cols] = new
            later[:, cols] = new.astype(BF16)


def relax_kernel(step_size, rows, weights, biases, inputs, got, relaxed, sent, even, odd):
    first = lax.axis_index("layer") == 0

    @pl.when(first)
    def _():
        relaxed[...] = inputs[...]

    @pl.when(jnp.logical_not(first))
    def _():
        relaxed[...] = got[...].astype(F32)

    even[...] = relaxed[...].astype(BF16)
    run_layers(range(4), step_size, weights, biases, relaxed, (even, odd))
    sent[:rows, :] = even[...]
    bias = biases[0:1, :]
    high = bias.astype(BF16)
    rest = bias - high.astype(F32)
    middle = rest.astype(BF16)
    low = (rest - middle.astype(F32)).astype(BF16)
    at = lax.broadcasted_iota(jnp.int32, (EXTRA, bias.shape[1]), 0)
    parts = jnp.where(at == 0, high.astype(F32), jnp.where(at == 1, middle.astype(F32), low.astype(F32)))
    sent[rows:, :] = jnp.where(at < 3, parts, 0.0).astype(BF16)


def ahead_kernel(step_size, rows, weights, biases, inputs, got, start, forcing, pair_bias, top, sent_forcing, state, even, odd):
    first = lax.axis_index("layer") == 0

    @pl.when(first)
    def _():
        start[...] = inputs[...]

    @pl.when(jnp.logical_not(first))
    def _():
        start[...] = got[:rows, :].astype(F32)

    even[...] = start[...].astype(BF16)
    bias = biases[0:1, :]
    for cols in tiles(state.shape[1]):
        slope = layer_of(even, weights.at[0], bias, cols)
        new = start[:, cols] + step_size * slope
        state[:, cols] = new
        odd[:, cols] = new.astype(BF16)
        forcing[:, cols] = start[:, cols] + (4.0 * step_size) * slope
    run_layers((1, 2, 3), step_size, weights, biases, state, (even, odd))
    top[...] = jnp.where(first, inputs[...].astype(BF16), even[...])
    difference = state[...] - forcing[...]
    forcing[...] = difference
    sent_forcing[...] = difference.astype(BF16)
    tail = got[rows:, :].astype(F32)
    pair_bias[...] = jnp.broadcast_to(tail[0:1, :] + (tail[1:2, :] + tail[2:3, :]), pair_bias.shape)


def coarse_kernel(chosen, factor, weights, biases, forcing, pair_weight, pair_bias, pair_forcing, got, before, mid, *rest):
    even, odd = rest[-2:]
    here = lax.axis_index("layer")

    taken = chosen(here % 4, here // 4)

    @pl.when(jnp.logical_not(taken))
    def _():
        for top in rest[:-2]:
            top[...] = before[...]

    @pl.when(taken)
    def _():
        even[...] = got[...]
        for cols in tiles(mid.shape[1]):
            slope = layer_of(even, pair_weight, pair_bias[0:1, :], cols)
            new = got[:, cols].astype(F32) + factor * slope + pair_forcing[:, cols].astype(F32)
            mid[:, cols] = new
            odd[:, cols] = new.astype(BF16)
        bias = biases[0:1, :]
        for top in rest[:-2]:
            for cols in tiles(mid.shape[1]):
                slope = layer_of(odd, weights.at[0], bias, cols)
                top[:, cols] = (mid[:, cols] + factor * slope + forcing[:, cols]).astype(BF16)


def held_kernel(got_1, got_2, got_3, held):
    here = lax.axis_index("layer")
    low, early = here % 4 < 2, here // 4 == 0
    held[...] = jnp.where(low, got_2[...], jnp.where(early, got_1[...], got_3[...]))


def final_kernel(step_size, weights, biases, inputs, one, down, low_mid, first_mid, high_mid, forcing, relaxed, left, state, coarse, even, odd):
    here = lax.axis_index("layer")
    slot, group = here % 4, here // 4

    def start_from(condition, source):
        @pl.when(condition)
        def _():
            state[...] = source[...].astype(F32)

    start_from(here == 0, inputs)
    start_from(here == 1, one)
    start_from((here > 0) & (here % 2 == 0), down)
    start_from((slot == 1) & (group > 0), low_mid)
    start_from((slot == 3) & (group == 0), first_mid)
    start_from((slot == 3) & (group > 0), high_mid)
    even[...] = state[...].astype(BF16)
    bias = biases[0:1, :]
    for cols in tiles(state.shape[1]):
        slope = layer_of(even, weights.at[0], bias, cols)
        old = state[:, cols]
        new = old + step_size * slope
        coarse[:, cols] = old + (4.0 * step_size) * slope + forcing[:, cols] - relaxed[:, cols]
        state[:, cols] = new
        odd[:, cols] = new.astype(BF16)
    run_layers((1, 2), step_size, weights, biases, state, (even, odd))
    left[...] = odd[...]


def last_kernel(step_size, weights, biases, left, state, new_states):
    bias = biases[3:4, :]
    for cols in tiles(state.shape[1]):
        new_states[:, cols] = state[:, cols] + step_size * layer_of(left, weights.at[3], bias, cols)


def gradient(step_size, weights, biases, left, adjoint, deltas, width):
    cols = pl.ds(pl.multiple_of(lax.axis_index("dp") * width, width), width)
    slope = jnp.tanh(jnp.dot(left[...], weights[3, :, cols], preferred_element_type=F32) + biases[3:4, cols])
    deltas[...] = (adjoint[...].astype(F32) * step_size * (1.0 - slope * slope)).astype(BF16)
    return lax.dot_general(left[...], deltas[...], (((0,), (0,)), ((), ())), preferred_element_type=F32)


def own_gradient_kernel(step_size, weights, biases, left, adjoint, total, deltas):
    total[...] = gradient(step_size, weights, biases, left, adjoint, deltas, total.shape[1])


def far_kernel(step_size, rows, count, weights, biases, pair_weight, pair_bias, total, *refs):
    far, down, forcings, adjoints = (refs[i * count : (i + 1) * count] for i in range(4))
    result, state, even, odd, adjoint, deltas = refs[4 * count :]
    is_odd = lax.axis_index("layer") % 2 == 1
    places = [slice(i * rows, (i + 1) * rows) for i in range(count)]

    @pl.when(is_odd)
    def _():
        for place, source in zip(places, far):
            odd[place, :] = source[...]
        for cols in tiles(state.shape[1]):
            slope = layer_of(odd, pair_weight, pair_bias[0:1, :], cols)
            for place, added in zip(places, forcings):
                new = odd[place, cols].astype(F32) + (4.0 * step_size) * slope[place, :] + added[:, cols].astype(F32)
                state[place, cols] = new
                even[place, cols] = new.astype(BF16)

    @pl.when(jnp.logical_not(is_odd))
    def _():
        for place, source in zip(places, down):
            state[place, :] = source[...].astype(F32)
            even[place, :] = source[...]

    for place, source in zip(places, adjoints):
        adjoint[place, :] = source[...]
    run_layers((0, 1, 2), step_size, weights, biases, state, (even, odd))
    result[...] = total[...] + gradient(step_size, weights, biases, odd, adjoint, deltas, result.shape[1])


def single_kernel(factor, weights, biases, got, added, out):
    for cols in tiles(out.shape[1]):
        slope = layer_of(got, weights.at[0], biases[0:1, :], cols)
        out[:, cols] = got[:, cols].astype(F32) + factor * slope + added[:, cols]


def pick_kernel(chosen, new, old, out):
    here = lax.axis_index("layer")
    out[...] = jnp.where(chosen(here % 4, here // 4), new[...], old[...])


def body(inputs, guesses, weights, biases, adjoint):
    blocks = lax.axis_size("layer")
    parts = lax.axis_size("dp")
    groups = blocks // 4
    step_size = 4.0 / (4 * blocks)
    rows, depth = inputs.shape
    width = depth // parts
    layer_flops = 2 * rows * depth * depth

    def along(state, pairs):
        return lax.ppermute(state, "layer", pairs)

    def across(state, pairs, by):
        flat = [(i * parts + z, j * parts + (z + by) % parts) for i, j in pairs for z in range(parts)]
        return lax.ppermute(state, ("layer", "dp"), flat)

    def shifted(array, by):
        return lax.ppermute(array, "dp", [(i, (i + by) % parts) for i in range(parts)])

    up = [(i, i + 1) for i in range(blocks - 1)]
    up_pair = [(i, i + 1) for i in range(0, blocks, 2)]
    down_pair = [(i + 1, i) for i in range(0, blocks, 2)]
    rounded = [pltpu.VMEM((rows, depth), BF16)] * 2

    guess_sent = call(round_kernel, plain((rows, depth), BF16), guesses[0])
    guess_prev = along(guess_sent, up)
    guess_sent, weights = lax.optimization_barrier((guess_sent, weights))
    held_weights, coarse_weight = call(
        load_kernel, (kept(weights), plain((depth, depth), BF16)), pltpu.with_memory_space_constraint(weights, pltpu.HBM),
        scratch=[pltpu.SemaphoreType.DMA((weights.shape[0] * 4 + 1,))], specs=[BULK],
    )
    guess_prev, coarse_weight = lax.optimization_barrier((guess_prev, coarse_weight))
    pair_weight = along(coarse_weight, up_pair)
    sent_adjoints = call(
        functools.partial(columns_kernel, parts), (plain((rows, width), BF16),) * parts, adjoint[0]
    )
    relaxed, relaxed_sent = call(
        functools.partial(relax_kernel, step_size, rows),
        (kept(inputs), plain((rows + EXTRA, depth), BF16)),
        held_weights, biases, inputs, guess_prev,
        scratch=rounded, flops=4 * layer_flops,
    )
    relaxed_got = along(relaxed_sent, up)
    start, forcing, pair_bias, ahead, forcing_sent = call(
        functools.partial(ahead_kernel, step_size, rows),
        (kept(inputs), kept(inputs), pltpu.VMEM((8, depth), F32), plain((rows, depth), BF16), plain((rows, depth), BF16)),
        held_weights, biases, inputs, relaxed_got,
        scratch=[pltpu.VMEM((rows, depth), F32)] + rounded, flops=4 * layer_flops,
    )
    pair_forcing = along(forcing_sent, up_pair)
    far_forcings = [across(forcing_sent, up_pair, by) for by in range(1, parts)]

    def two_steps(top, pairs, chosen, last=False, beside=()):
        got, *_ = lax.optimization_barrier((along(top, pairs), *beside))
        mid, *new_top = call(
            functools.partial(coarse_kernel, chosen, 4.0 * step_size),
            (kept(inputs),) if last else (kept(inputs), plain((rows, depth), BF16)),
            held_weights, biases, forcing, pair_weight, pair_bias, pair_forcing, got, top,
            scratch=rounded, flops=2 * layer_flops,
        )
        return got, mid, *new_top

    here = lax.axis_index("layer")
    slot, group = here % 4, here // 4
    last_group = groups - 1

    def single(factor, got, added):
        return call(
            functools.partial(single_kernel, factor), plain((rows, depth), F32),
            held_weights, biases, got, added, flops=layer_flops,
        )

    def finish(gots, mids):
        got_1, got_2, got_3 = gots
        mid_1, mid_2, mid_3 = mids
        held = call(held_kernel, plain((rows, depth), BF16), got_1, got_2, got_3)
        down = along(held, down_pair)
        return call(
            functools.partial(final_kernel, step_size),
            (plain((rows, depth), BF16), kept(inputs), plain((rows, depth), F32)),
            held_weights, biases, inputs, start, down, mid_2, mid_1, mid_3, forcing, relaxed,
            scratch=rounded, flops=3 * layer_flops,
        )

    top_0 = ahead
    if groups > 2:
        after = single(4.0 * step_size, along(ahead, up_pair), forcing)
        top_0 = jnp.where((slot == 1) & (group > 0), after.astype(BF16), ahead)
    got_1, mid_1, top_1 = two_steps(
        top_0, [(4 * m + 1, 4 * m + 3) for m in range(groups - 1)], lambda slot, group: (slot == 3) & (group < last_group)
    )
    top_1, *sent_adjoints = lax.optimization_barrier((top_1, *sent_adjoints))
    adjoints = sent_adjoints[:1] + [shifted(sent_adjoints[by], by) for by in range(1, parts)]
    got_2, mid_2, top_2 = two_steps(
        top_1, [(4 * m - 1, 4 * m + 1) for m in range(1, groups)], lambda slot, group: (slot == 1) & (group > 0),
        beside=adjoints,
    )
    top_2, *far_forcings = lax.optimization_barrier((top_2, *far_forcings))
    got_3, mid_3 = two_steps(
        top_2, [(4 * m + 1, 4 * m + 3) for m in range(1, groups)], lambda slot, group: (slot == 3) & (group > 0), True
    )
    left, state, coarse_states = finish((got_1, got_2, got_3), (mid_1, mid_2, mid_3))
    if groups > 2:
        late = lambda slot, group: group > 1
        relaxed_out = call(functools.partial(pick_kernel, late), plain((rows, depth), F32), relaxed, relaxed)
        solved = coarse_states + relaxed_out
        below = along(top_1, [(4 * m - 1, 4 * m + 3) for m in range(2, groups)])
        base = solved - single(16.0 * step_size, below, jnp.zeros((rows, depth), F32))
        for m in range(2, groups):
            new = single(16.0 * step_size, along(solved.astype(BF16), [(4 * m - 1, 4 * m + 3)]), base)
            solved = jnp.where(here == 4 * m + 3, new, solved)
        new_2, new_mid_2, top_2 = two_steps(
            jnp.where(slot == 3, solved.astype(BF16), top_2), [(4 * m - 1, 4 * m + 1) for m in range(2, groups)], lambda slot, group: (slot == 1) & (group > 1)
        )
        new_3, new_mid_3 = two_steps(
            top_2, [(4 * m + 1, 4 * m + 3) for m in range(2, groups)], lambda slot, group: (slot == 3) & (group > 1), True
        )
        mids = [
            call(functools.partial(pick_kernel, late), kept(inputs), new, old)
            for new, old in ((new_mid_2, mid_2), (new_mid_3, mid_3))
        ]
        gots = [jnp.where(group > 1, new, old) for new, old in ((new_2, got_2), (new_3, got_3))]
        left, state, coarse_early = finish((got_1, *gots), (mid_1, *mids))
        coarse_states = jnp.where(slot == 3, solved - relaxed_out, coarse_states)
    leaps = [(0, 1)] + [(i, i + 2) for i in range(1, blocks - 2, 2)]
    far = [across(top_2, leaps, by) for by in range(1, parts)]
    left, *far = lax.optimization_barrier((left, *far))
    far_down = [along(state_far, down_pair) for state_far in far]
    new_states = call(
        functools.partial(last_kernel, step_size), plain((rows, depth), F32),
        held_weights, biases, left, state, flops=layer_flops,
    )
    total = call(
        functools.partial(own_gradient_kernel, step_size), pltpu.VMEM((depth, width), F32),
        held_weights, biases, left, adjoints[0], scratch=[pltpu.VMEM((rows, width), BF16)], flops=layer_flops,
    )
    others = (parts - 1) * rows
    weight_grad = call(
        functools.partial(far_kernel, step_size, rows, parts - 1), plain((depth, width), F32),
        held_weights, biases, pair_weight, pair_bias, total, *far, *far_down, *far_forcings, *adjoints[1:],
        scratch=[pltpu.VMEM((others, depth), F32)] + [pltpu.VMEM((others, depth), BF16)] * 2
        + [pltpu.VMEM((others, width), BF16)] * 2,
        flops=6 * (parts - 1) * layer_flops,
    )
    return (new_states[None], coarse_states[None], weight_grad[None])


def solution(mesh):
    return jax.shard_map(
        body,
        mesh=mesh,
        in_specs=(
            P("dp", None),
            P("layer", "dp", None),
            P("layer", None, None),
            P("layer", None),
            P("layer", "dp", None),
        ),
        out_specs=(P("layer", "dp", None), P("layer", "dp", None), P("layer", None, "dp")),
        check_vma=False,
    )
```

```python
import functools

import jax
import jax.numpy as jnp
from jax import lax
from jax.experimental import pallas as pl
from jax.experimental.pallas import tpu as pltpu
from jax.sharding import PartitionSpec as P

BF16 = jnp.bfloat16
F32 = jnp.float32
TILE = 256
EXTRA = 16
WHOLE = pl.BlockSpec(memory_space=pltpu.VMEM)
BULK = pl.BlockSpec(memory_space=pltpu.HBM)


def call(kernel, outs, *args, scratch=(), flops=0, specs=None):
    moved = sum(a.size * a.dtype.itemsize for a in args)
    return pl.pallas_call(
        kernel,
        out_shape=outs,
        in_specs=specs or [WHOLE] * len(args),
        out_specs=jax.tree.map(lambda _: WHOLE, outs, is_leaf=lambda leaf: not isinstance(leaf, (tuple, list))),
        scratch_shapes=list(scratch),
        compiler_params=pltpu.CompilerParams(vmem_limit_bytes=8 << 20),
        cost_estimate=pl.CostEstimate(flops=flops, bytes_accessed=moved, transcendentals=0),
    )(*args)


def kept(like, dtype=None):
    return pltpu.VMEM(like.shape, dtype or like.dtype)


def plain(shape, dtype):
    return jax.ShapeDtypeStruct(shape, dtype)


def tiles(width):
    step = min(TILE, width)
    return [slice(at, at + step) for at in range(0, width, step)]


def layer_of(rounded_ref, weight_ref, bias, cols):
    product = jnp.dot(rounded_ref[...], weight_ref[:, cols], preferred_element_type=F32)
    return jnp.tanh(product + bias[:, cols])


def round_kernel(guess, sent_guess):
    sent_guess[...] = guess[...].astype(BF16)


def columns_kernel(parts, adjoint, *columns):
    width = adjoint.shape[1] // parts
    for by, target in enumerate(columns):
        index = lax.rem(lax.axis_index("dp") + by, parts)
        target[...] = adjoint[:, pl.ds(pl.multiple_of(index * width, width), width)]


def load_kernel(source, target, coarse_weight, sems):
    layers, depth = source.shape[:2]
    pieces = (sems.shape[0] - 1) // layers
    step = depth // pieces
    copies = [
        pltpu.make_async_copy(
            source.at[i, pl.ds(at * step, step)], target.at[i, pl.ds(at * step, step)], sems.at[i * pieces + at]
        )
        for i in range(layers)
        for at in range(pieces)
    ]
    for copy in copies:
        copy.start()
    for copy in copies[:pieces]:
        copy.wait()
    again = pltpu.make_async_copy(target.at[0], coarse_weight, sems.at[layers * pieces])
    again.start()
    for copy in copies[pieces:]:
        copy.wait()
    again.wait()


def run_layers(layers, step_size, weights, biases, state, rounded):
    for layer in layers:
        bias = biases[layer : layer + 1, :]
        now, later = rounded[layer % 2], rounded[(layer + 1) % 2]
        for cols in tiles(state.shape[1]):
            new = state[:, cols] + step_size * layer_of(now, weights.at[layer], bias, cols)
            state[:, cols] = new
            later[:, cols] = new.astype(BF16)


def relax_kernel(step_size, rows, weights, biases, inputs, got, relaxed, sent, even, odd):
    first = lax.axis_index("layer") == 0

    @pl.when(first)
    def _():
        relaxed[...] = inputs[...]

    @pl.when(jnp.logical_not(first))
    def _():
        relaxed[...] = got[...].astype(F32)

    even[...] = relaxed[...].astype(BF16)
    run_layers(range(4), step_size, weights, biases, relaxed, (even, odd))
    sent[:rows, :] = even[...]
    bias = biases[0:1, :]
    high = bias.astype(BF16)
    rest = bias - high.astype(F32)
    middle = rest.astype(BF16)
    low = (rest - middle.astype(F32)).astype(BF16)
    at = lax.broadcasted_iota(jnp.int32, (EXTRA, bias.shape[1]), 0)
    parts = jnp.where(at == 0, high.astype(F32), jnp.where(at == 1, middle.astype(F32), low.astype(F32)))
    sent[rows:, :] = jnp.where(at < 3, parts, 0.0).astype(BF16)


def ahead_kernel(step_size, rows, weights, biases, inputs, got, start, forcing, pair_bias, top, sent_forcing, state, even, odd):
    first = lax.axis_index("layer") == 0

    @pl.when(first)
    def _():
        start[...] = inputs[...]

    @pl.when(jnp.logical_not(first))
    def _():
        start[...] = got[:rows, :].astype(F32)

    even[...] = start[...].astype(BF16)
    bias = biases[0:1, :]
    for cols in tiles(state.shape[1]):
        slope = layer_of(even, weights.at[0], bias, cols)
        new = start[:, cols] + step_size * slope
        state[:, cols] = new
        odd[:, cols] = new.astype(BF16)
        forcing[:, cols] = start[:, cols] + (4.0 * step_size) * slope
    run_layers((1, 2, 3), step_size, weights, biases, state, (even, odd))
    top[...] = even[...]
    difference = state[...] - forcing[...]
    forcing[...] = difference
    sent_forcing[...] = difference.astype(BF16)
    tail = got[rows:, :].astype(F32)
    pair_bias[...] = jnp.broadcast_to(tail[0:1, :] + (tail[1:2, :] + tail[2:3, :]), pair_bias.shape)


def coarse_kernel(chosen, factor, weights, biases, forcing, pair_weight, pair_bias, pair_forcing, got, mid, *rest):
    even, odd = rest[-2:]
    here = lax.axis_index("layer")


    @pl.when(chosen(here % 4, here // 4))
    def _():
        even[...] = got[...]
        for cols in tiles(mid.shape[1]):
            slope = layer_of(even, pair_weight, pair_bias[0:1, :], cols)
            new = got[:, cols].astype(F32) + factor * slope + pair_forcing[:, cols].astype(F32)
            mid[:, cols] = new
            odd[:, cols] = new.astype(BF16)
        bias = biases[0:1, :]
        for top in rest[:-2]:
            for cols in tiles(mid.shape[1]):
                slope = layer_of(odd, weights.at[0], bias, cols)
                top[:, cols] = (mid[:, cols] + factor * slope + forcing[:, cols]).astype(BF16)


def held_kernel(got_1, got_2, got_3, held):
    here = lax.axis_index("layer")
    low, early = here % 4 < 2, here // 4 == 0
    held[...] = jnp.where(low, got_2[...], jnp.where(early, got_1[...], got_3[...]))


def final_kernel(step_size, weights, biases, inputs, one, down, low_mid, first_mid, high_mid, forcing, relaxed, left, state, coarse, even, odd):
    here = lax.axis_index("layer")
    slot, group = here % 4, here // 4

    def start_from(condition, source):
        @pl.when(condition)
        def _():
            state[...] = source[...].astype(F32)

    start_from(here == 0, inputs)
    start_from(here == 1, one)
    start_from((here > 0) & (here % 2 == 0), down)
    start_from((slot == 1) & (group > 0), low_mid)
    start_from((slot == 3) & (group == 0), first_mid)
    start_from((slot == 3) & (group > 0), high_mid)
    even[...] = state[...].astype(BF16)
    bias = biases[0:1, :]
    for cols in tiles(state.shape[1]):
        slope = layer_of(even, weights.at[0], bias, cols)
        old = state[:, cols]
        new = old + step_size * slope
        coarse[:, cols] = old + (4.0 * step_size) * slope + forcing[:, cols] - relaxed[:, cols]
        state[:, cols] = new
        odd[:, cols] = new.astype(BF16)
    run_layers((1, 2), step_size, weights, biases, state, (even, odd))
    left[...] = odd[...]


def last_kernel(step_size, weights, biases, left, state, new_states):
    bias = biases[3:4, :]
    for cols in tiles(state.shape[1]):
        new_states[:, cols] = state[:, cols] + step_size * layer_of(left, weights.at[3], bias, cols)


def gradient(step_size, weights, biases, left, adjoint, deltas, width):
    cols = pl.ds(pl.multiple_of(lax.axis_index("dp") * width, width), width)
    slope = jnp.tanh(jnp.dot(left[...], weights[3, :, cols], preferred_element_type=F32) + biases[3:4, cols])
    deltas[...] = (adjoint[...].astype(F32) * step_size * (1.0 - slope * slope)).astype(BF16)
    return lax.dot_general(left[...], deltas[...], (((0,), (0,)), ((), ())), preferred_element_type=F32)


def gradient_kernel(step_size, conditions, has_total, weights, biases, *refs):
    count = len(conditions)
    lefts, adjoints, (total, deltas) = refs[:count], refs[count : 2 * count], refs[-2:]
    place = lax.axis_index("dp")
    if has_total:
        total[...] = refs[2 * count][...]
    for i, (left, adjoint, condition) in enumerate(zip(lefts, adjoints, conditions)):
        if i == 0 and not has_total:
            total[...] = gradient(step_size, weights, biases, left, adjoint, deltas, total.shape[1])
        else:

            @pl.when(condition(place))
            def _(left=left, adjoint=adjoint):
                total[...] += gradient(step_size, weights, biases, left, adjoint, deltas, total.shape[1])


def single_kernel(factor, weights, biases, got, added, out):
    for cols in tiles(out.shape[1]):
        slope = layer_of(got, weights.at[0], biases[0:1, :], cols)
        out[:, cols] = got[:, cols].astype(F32) + factor * slope + added[:, cols]


def pick_kernel(chosen, new, old, out):
    here = lax.axis_index("layer")
    out[...] = jnp.where(chosen(here % 4, here // 4), new[...], old[...])


def body(inputs, guesses, weights, biases, adjoint):
    blocks = lax.axis_size("layer")
    parts = lax.axis_size("dp")
    groups = blocks // 4
    step_size = 4.0 / (4 * blocks)
    rows, depth = inputs.shape
    width = depth // parts
    layer_flops = 2 * rows * depth * depth

    def along(state, pairs):
        return lax.ppermute(state, "layer", pairs)

    def shifted(array, by):
        return lax.ppermute(array, "dp", [(i, (i + by) % parts) for i in range(parts)])

    up = [(i, i + 1) for i in range(blocks - 1)]
    up_pair = [(i, i + 1) for i in range(0, blocks, 2)]
    down_pair = [(i + 1, i) for i in range(0, blocks, 2)]
    rounded = [pltpu.VMEM((rows, depth), BF16)] * 2

    guess_sent = call(round_kernel, plain((rows, depth), BF16), guesses[0])
    guess_prev = along(guess_sent, up)
    guess_sent, weights = lax.optimization_barrier((guess_sent, weights))
    held_weights, coarse_weight = call(
        load_kernel, (kept(weights), plain((depth, depth), BF16)), pltpu.with_memory_space_constraint(weights, pltpu.HBM),
        scratch=[pltpu.SemaphoreType.DMA((weights.shape[0] * 4 + 1,))], specs=[BULK],
    )
    guess_prev, coarse_weight = lax.optimization_barrier((guess_prev, coarse_weight))
    pair_weight = along(coarse_weight, up_pair)
    sent_adjoints = call(
        functools.partial(columns_kernel, parts), (plain((rows, width), BF16),) * parts, adjoint[0]
    )
    relaxed, relaxed_sent = call(
        functools.partial(relax_kernel, step_size, rows),
        (kept(inputs), plain((rows + EXTRA, depth), BF16)),
        held_weights, biases, inputs, guess_prev,
        scratch=rounded, flops=4 * layer_flops,
    )
    relaxed_got = along(relaxed_sent, up)
    start, forcing, pair_bias, ahead, forcing_sent = call(
        functools.partial(ahead_kernel, step_size, rows),
        (kept(inputs), kept(inputs), pltpu.VMEM((8, depth), F32), plain((rows, depth), BF16), plain((rows, depth), BF16)),
        held_weights, biases, inputs, relaxed_got,
        scratch=[pltpu.VMEM((rows, depth), F32)] + rounded, flops=4 * layer_flops,
    )
    pair_forcing = along(forcing_sent, up_pair)

    def two_steps(top, pairs, chosen, last=False, beside=()):
        got, *_ = lax.optimization_barrier((along(top, pairs), *beside))
        mid, *new_top = call(
            functools.partial(coarse_kernel, chosen, 4.0 * step_size),
            (kept(inputs),) if last else (kept(inputs), plain((rows, depth), BF16)),
            held_weights, biases, forcing, pair_weight, pair_bias, pair_forcing, got,
            scratch=rounded, flops=2 * layer_flops,
        )
        return got, mid, *new_top

    here = lax.axis_index("layer")
    slot, group = here % 4, here // 4
    last_group = groups - 1

    def single(factor, got, added):
        return call(
            functools.partial(single_kernel, factor), plain((rows, depth), F32),
            held_weights, biases, got, added, flops=layer_flops,
        )

    def finish(gots, mids):
        got_1, got_2, got_3 = gots
        mid_1, mid_2, mid_3 = mids
        held = call(held_kernel, plain((rows, depth), BF16), got_1, got_2, got_3)
        down = along(held, down_pair)
        return call(
            functools.partial(final_kernel, step_size),
            (plain((rows, depth), BF16), kept(inputs), plain((rows, depth), F32)),
            held_weights, biases, inputs, start, down, mid_2, mid_1, mid_3, forcing, relaxed,
            scratch=rounded, flops=3 * layer_flops,
        )

    top_0 = ahead
    if groups > 2:
        after = single(4.0 * step_size, along(ahead, up_pair), forcing)
        top_0 = jnp.where((slot == 1) & (group > 0), after.astype(BF16), ahead)
    got_1, mid_1, top_1 = two_steps(
        top_0, [(4 * m + 1, 4 * m + 3) for m in range(groups - 1)], lambda slot, group: (slot == 3) & (group < last_group)
    )
    top_1, *sent_adjoints = lax.optimization_barrier((top_1, *sent_adjoints))
    adjoints = sent_adjoints[:1] + [shifted(sent_adjoints[by], by) for by in range(1, parts)]
    got_2, mid_2, top_2 = two_steps(
        top_1, [(4 * m - 1, 4 * m + 1) for m in range(1, groups)], lambda slot, group: (slot == 1) & (group > 0),
        beside=adjoints,
    )
    got_3, mid_3 = two_steps(
        top_2, [(4 * m + 1, 4 * m + 3) for m in range(1, groups)], lambda slot, group: (slot == 3) & (group > 0), True
    )
    left, state, coarse_states = finish((got_1, got_2, got_3), (mid_1, mid_2, mid_3))
    if groups > 2:
        late = lambda slot, group: group > 1
        relaxed_out = call(functools.partial(pick_kernel, late), plain((rows, depth), F32), relaxed, relaxed)
        solved = coarse_states + relaxed_out
        below = along(top_1, [(4 * m - 1, 4 * m + 3) for m in range(2, groups)])
        base = solved - single(16.0 * step_size, below, jnp.zeros((rows, depth), F32))
        for m in range(2, groups):
            new = single(16.0 * step_size, along(solved.astype(BF16), [(4 * m - 1, 4 * m + 3)]), base)
            solved = jnp.where(here == 4 * m + 3, new, solved)
        new_2, new_mid_2, top_2 = two_steps(
            solved.astype(BF16), [(4 * m - 1, 4 * m + 1) for m in range(2, groups)], lambda slot, group: (slot == 1) & (group > 1)
        )
        new_3, new_mid_3 = two_steps(
            top_2, [(4 * m + 1, 4 * m + 3) for m in range(2, groups)], lambda slot, group: (slot == 3) & (group > 1), True
        )
        mids = [
            call(functools.partial(pick_kernel, late), kept(inputs), new, old)
            for new, old in ((new_mid_2, mid_2), (new_mid_3, mid_3))
        ]
        gots = [jnp.where(group > 1, new, old) for new, old in ((new_2, got_2), (new_3, got_3))]
        left, state, coarse_early = finish((got_1, *gots), (mid_1, *mids))
        coarse_states = jnp.where(slot == 3, solved - relaxed_out, coarse_states)
    def along_dp(array, pairs):
        return lax.ppermute(array, "dp", pairs)

    right = [(i, i + 1) for i in range(parts - 1)]
    back = [(i + 1, i) for i in range(parts - 1)]
    from_left, from_right = along_dp(left, right), along_dp(left, back)
    beyond = []
    for by in range(3, parts):
        onward, home = [(i, i + by) for i in range(parts - by)], [(i + by, i) for i in range(parts - by)]
        if 2 * by >= parts:
            ahead_rows = behind_rows = along_dp(left, onward + home)
        else:
            ahead_rows, behind_rows = along_dp(left, onward), along_dp(left, home)
        beyond.append((ahead_rows, adjoints[by], lambda place, by=by: place >= by))
        beyond.append((behind_rows, adjoints[parts - by], lambda place, by=by: place < parts - by))
    beyond.append((along_dp(from_left, right[1:]), adjoints[2 % parts], lambda place: place >= 2))
    beyond.append((along_dp(from_right, back[:-1]), adjoints[-2], lambda place: place < parts - 2))
    new_states = call(
        functools.partial(last_kernel, step_size), plain((rows, depth), F32),
        held_weights, biases, left, state, flops=layer_flops,
    )

    def add_up(out, blocks_of_rows, total=()):
        datas, columns, conditions = zip(*blocks_of_rows)
        return call(
            functools.partial(gradient_kernel, step_size, conditions, bool(total)), out,
            held_weights, biases, *datas, *columns, *total,
            scratch=[pltpu.VMEM((rows, width), BF16)], flops=len(datas) * layer_flops // 2,
        )

    near = [
        (left, adjoints[0], None),
        (from_left, adjoints[1], lambda place: place >= 1),
        (from_right, adjoints[-1], lambda place: place < parts - 1),
    ]
    total = add_up(pltpu.VMEM((depth, width), F32), near)
    weight_grad = add_up(plain((depth, width), F32), beyond, (total,))
    return (new_states[None], coarse_states[None], weight_grad[None])


def solution(mesh):
    return jax.shard_map(
        body,
        mesh=mesh,
        in_specs=(
            P("dp", None),
            P("layer", "dp", None),
            P("layer", None, None),
            P("layer", None),
            P("layer", "dp", None),
        ),
        out_specs=(P("layer", "dp", None), P("layer", "dp", None), P("layer", None, "dp")),
        check_vma=False,
    )
```

```python
import functools

import jax
import jax.numpy as jnp
from jax import lax
from jax.experimental import pallas as pl
from jax.experimental.pallas import tpu as pltpu
from jax.sharding import PartitionSpec as P

BF16 = jnp.bfloat16
F32 = jnp.float32
TILE = 256
EXTRA = 16
WHOLE = pl.BlockSpec(memory_space=pltpu.VMEM)
BULK = pl.BlockSpec(memory_space=pltpu.HBM)


def call(kernel, outs, *args, scratch=(), flops=0, specs=None):
    moved = sum(a.size * a.dtype.itemsize for a in args)
    return pl.pallas_call(
        kernel,
        out_shape=outs,
        in_specs=specs or [WHOLE] * len(args),
        out_specs=jax.tree.map(lambda _: WHOLE, outs, is_leaf=lambda leaf: not isinstance(leaf, (tuple, list))),
        scratch_shapes=list(scratch),
        compiler_params=pltpu.CompilerParams(vmem_limit_bytes=8 << 20),
        cost_estimate=pl.CostEstimate(flops=flops, bytes_accessed=moved, transcendentals=0),
    )(*args)


def kept(like, dtype=None):
    return pltpu.VMEM(like.shape, dtype or like.dtype)


def plain(shape, dtype):
    return jax.ShapeDtypeStruct(shape, dtype)


def tiles(width):
    step = min(TILE, width)
    return [slice(at, at + step) for at in range(0, width, step)]


def layer_of(rounded_ref, weight_ref, bias, cols):
    product = jnp.dot(rounded_ref[...], weight_ref[:, cols], preferred_element_type=F32)
    return jnp.tanh(product + bias[:, cols])


def round_kernel(guess, sent_guess):
    sent_guess[...] = guess[...].astype(BF16)


def columns_kernel(parts, adjoint, *columns):
    width = adjoint.shape[1] // parts
    for by, target in enumerate(columns):
        index = lax.rem(lax.axis_index("dp") + by, parts)
        target[...] = adjoint[:, pl.ds(pl.multiple_of(index * width, width), width)]


def load_kernel(source, target, coarse_weight, sems):
    layers, depth = source.shape[:2]
    pieces = (sems.shape[0] - 1) // layers
    step = depth // pieces
    copies = [
        pltpu.make_async_copy(
            source.at[i, pl.ds(at * step, step)], target.at[i, pl.ds(at * step, step)], sems.at[i * pieces + at]
        )
        for i in range(layers)
        for at in range(pieces)
    ]
    for copy in copies:
        copy.start()
    for copy in copies[:pieces]:
        copy.wait()
    again = pltpu.make_async_copy(target.at[0], coarse_weight, sems.at[layers * pieces])
    again.start()
    for copy in copies[pieces:]:
        copy.wait()
    again.wait()


def run_layers(layers, step_size, weights, biases, state, rounded):
    for layer in layers:
        bias = biases[layer : layer + 1, :]
        now, later = rounded[layer % 2], rounded[(layer + 1) % 2]
        for cols in tiles(state.shape[1]):
            new = state[:, cols] + step_size * layer_of(now, weights.at[layer], bias, cols)
            state[:, cols] = new
            later[:, cols] = new.astype(BF16)


def relax_kernel(step_size, rows, weights, biases, inputs, got, relaxed, sent, even, odd):
    first = lax.axis_index("layer") == 0

    @pl.when(first)
    def _():
        relaxed[...] = inputs[...]

    @pl.when(jnp.logical_not(first))
    def _():
        relaxed[...] = got[...].astype(F32)

    even[...] = relaxed[...].astype(BF16)
    run_layers(range(4), step_size, weights, biases, relaxed, (even, odd))
    sent[:rows, :] = even[...]
    bias = biases[0:1, :]
    high = bias.astype(BF16)
    rest = bias - high.astype(F32)
    middle = rest.astype(BF16)
    low = (rest - middle.astype(F32)).astype(BF16)
    at = lax.broadcasted_iota(jnp.int32, (EXTRA, bias.shape[1]), 0)
    parts = jnp.where(at == 0, high.astype(F32), jnp.where(at == 1, middle.astype(F32), low.astype(F32)))
    sent[rows:, :] = jnp.where(at < 3, parts, 0.0).astype(BF16)


def ahead_kernel(step_size, rows, weights, biases, inputs, got, start, forcing, pair_bias, top, sent_forcing, state, even, odd):
    first = lax.axis_index("layer") == 0

    @pl.when(first)
    def _():
        start[...] = inputs[...]

    @pl.when(jnp.logical_not(first))
    def _():
        start[...] = got[:rows, :].astype(F32)

    even[...] = start[...].astype(BF16)
    bias = biases[0:1, :]
    for cols in tiles(state.shape[1]):
        slope = layer_of(even, weights.at[0], bias, cols)
        new = start[:, cols] + step_size * slope
        state[:, cols] = new
        odd[:, cols] = new.astype(BF16)
        forcing[:, cols] = start[:, cols] + (4.0 * step_size) * slope
    run_layers((1, 2, 3), step_size, weights, biases, state, (even, odd))
    top[...] = jnp.where(first, inputs[...].astype(BF16), even[...])
    difference = state[...] - forcing[...]
    forcing[...] = difference
    sent_forcing[...] = difference.astype(BF16)
    tail = got[rows:, :].astype(F32)
    pair_bias[...] = jnp.broadcast_to(tail[0:1, :] + (tail[1:2, :] + tail[2:3, :]), pair_bias.shape)


def coarse_kernel(chosen, factor, weights, biases, forcing, pair_weight, pair_bias, pair_forcing, got, before, mid, *rest):
    even, odd = rest[-2:]
    here = lax.axis_index("layer")

    taken = chosen(here % 4, here // 4)

    @pl.when(jnp.logical_not(taken))
    def _():
        for top in rest[:-2]:
            top[...] = before[...]

    @pl.when(taken)
    def _():
        even[...] = got[...]
        for cols in tiles(mid.shape[1]):
            slope = layer_of(even, pair_weight, pair_bias[0:1, :], cols)
            new = got[:, cols].astype(F32) + factor * slope + pair_forcing[:, cols].astype(F32)
            mid[:, cols] = new
            odd[:, cols] = new.astype(BF16)
        bias = biases[0:1, :]
        for top in rest[:-2]:
            for cols in tiles(mid.shape[1]):
                slope = layer_of(odd, weights.at[0], bias, cols)
                top[:, cols] = (mid[:, cols] + factor * slope + forcing[:, cols]).astype(BF16)


def held_kernel(got_1, got_2, got_3, held):
    here = lax.axis_index("layer")
    low, early = here % 4 < 2, here // 4 == 0
    held[...] = jnp.where(low, got_2[...], jnp.where(early, got_1[...], got_3[...]))


def final_kernel(step_size, weights, biases, inputs, one, down, low_mid, first_mid, high_mid, forcing, relaxed, left, state, coarse, even, odd):
    here = lax.axis_index("layer")
    slot, group = here % 4, here // 4

    def start_from(condition, source):
        @pl.when(condition)
        def _():
            state[...] = source[...].astype(F32)

    start_from(here == 0, inputs)
    start_from(here == 1, one)
    start_from((here > 0) & (here % 2 == 0), down)
    start_from((slot == 1) & (group > 0), low_mid)
    start_from((slot == 3) & (group == 0), first_mid)
    start_from((slot == 3) & (group > 0), high_mid)
    even[...] = state[...].astype(BF16)
    bias = biases[0:1, :]
    for cols in tiles(state.shape[1]):
        slope = layer_of(even, weights.at[0], bias, cols)
        old = state[:, cols]
        new = old + step_size * slope
        coarse[:, cols] = old + (4.0 * step_size) * slope + forcing[:, cols] - relaxed[:, cols]
        state[:, cols] = new
        odd[:, cols] = new.astype(BF16)
    run_layers((1, 2), step_size, weights, biases, state, (even, odd))
    left[...] = odd[...]


def last_kernel(step_size, weights, biases, left, state, new_states):
    bias = biases[3:4, :]
    for cols in tiles(state.shape[1]):
        new_states[:, cols] = state[:, cols] + step_size * layer_of(left, weights.at[3], bias, cols)


def gradient(step_size, weights, biases, left, adjoint, deltas, width):
    cols = pl.ds(pl.multiple_of(lax.axis_index("dp") * width, width), width)
    slope = jnp.tanh(jnp.dot(left[...], weights[3, :, cols], preferred_element_type=F32) + biases[3:4, cols])
    deltas[...] = (adjoint[...].astype(F32) * step_size * (1.0 - slope * slope)).astype(BF16)
    return lax.dot_general(left[...], deltas[...], (((0,), (0,)), ((), ())), preferred_element_type=F32)


def own_gradient_kernel(step_size, weights, biases, left, adjoint, total, deltas):
    total[...] = gradient(step_size, weights, biases, left, adjoint, deltas, total.shape[1])


def even_kernel(step_size, rows, count, weights, biases, total, *refs):
    starts, adjoints = refs[:count], refs[count : 2 * count]
    result, state, even, odd, adjoint, deltas = refs[2 * count :]
    is_even = lax.axis_index("layer") % 2 == 0

    @pl.when(jnp.logical_not(is_even))
    def _():
        result[...] = total[...]

    @pl.when(is_even)
    def _():
        for i, (source, columns) in enumerate(zip(starts, adjoints)):
            place = slice(i * rows, (i + 1) * rows)
            state[place, :] = source[...].astype(F32)
            even[place, :] = source[...]
            adjoint[place, :] = columns[...]
        run_layers((0, 1, 2), step_size, weights, biases, state, (even, odd))
        result[...] = total[...] + gradient(step_size, weights, biases, odd, adjoint, deltas, result.shape[1])


def odd_kernel(step_size, count, weights, biases, total, *refs):
    lefts, adjoints = refs[:count], refs[count : 2 * count]
    result, deltas = refs[2 * count :]
    result[...] = total[...]

    @pl.when(lax.axis_index("layer") % 2 == 1)
    def _():
        for left, adjoint in zip(lefts, adjoints):
            result[...] += gradient(step_size, weights, biases, left, adjoint, deltas, result.shape[1])


def single_kernel(factor, weights, biases, got, added, out):
    for cols in tiles(out.shape[1]):
        slope = layer_of(got, weights.at[0], biases[0:1, :], cols)
        out[:, cols] = got[:, cols].astype(F32) + factor * slope + added[:, cols]


def pick_kernel(chosen, new, old, out):
    here = lax.axis_index("layer")
    out[...] = jnp.where(chosen(here % 4, here // 4), new[...], old[...])


def body(inputs, guesses, weights, biases, adjoint):
    blocks = lax.axis_size("layer")
    parts = lax.axis_size("dp")
    groups = blocks // 4
    step_size = 4.0 / (4 * blocks)
    rows, depth = inputs.shape
    width = depth // parts
    layer_flops = 2 * rows * depth * depth

    def along(state, pairs):
        return lax.ppermute(state, "layer", pairs)

    def across(state, pairs, by):
        flat = [(i * parts + z, j * parts + (z + by) % parts) for i, j in pairs for z in range(parts)]
        return lax.ppermute(state, ("layer", "dp"), flat)

    def shifted(array, by):
        return lax.ppermute(array, "dp", [(i, (i + by) % parts) for i in range(parts)])

    up = [(i, i + 1) for i in range(blocks - 1)]
    up_pair = [(i, i + 1) for i in range(0, blocks, 2)]
    down_pair = [(i + 1, i) for i in range(0, blocks, 2)]
    rounded = [pltpu.VMEM((rows, depth), BF16)] * 2

    guess_sent = call(round_kernel, plain((rows, depth), BF16), guesses[0])
    guess_prev = along(guess_sent, up)
    guess_sent, weights = lax.optimization_barrier((guess_sent, weights))
    held_weights, coarse_weight = call(
        load_kernel, (kept(weights), plain((depth, depth), BF16)), pltpu.with_memory_space_constraint(weights, pltpu.HBM),
        scratch=[pltpu.SemaphoreType.DMA((weights.shape[0] * 4 + 1,))], specs=[BULK],
    )
    guess_prev, coarse_weight = lax.optimization_barrier((guess_prev, coarse_weight))
    pair_weight = along(coarse_weight, up_pair)
    sent_adjoints = call(
        functools.partial(columns_kernel, parts), (plain((rows, width), BF16),) * parts, adjoint[0]
    )
    relaxed, relaxed_sent = call(
        functools.partial(relax_kernel, step_size, rows),
        (kept(inputs), plain((rows + EXTRA, depth), BF16)),
        held_weights, biases, inputs, guess_prev,
        scratch=rounded, flops=4 * layer_flops,
    )
    relaxed_got = along(relaxed_sent, up)
    start, forcing, pair_bias, ahead, forcing_sent = call(
        functools.partial(ahead_kernel, step_size, rows),
        (kept(inputs), kept(inputs), pltpu.VMEM((8, depth), F32), plain((rows, depth), BF16), plain((rows, depth), BF16)),
        held_weights, biases, inputs, relaxed_got,
        scratch=[pltpu.VMEM((rows, depth), F32)] + rounded, flops=4 * layer_flops,
    )
    pair_forcing = along(forcing_sent, up_pair)

    def two_steps(top, pairs, chosen, last=False, beside=()):
        got, *_ = lax.optimization_barrier((along(top, pairs), *beside))
        mid, *new_top = call(
            functools.partial(coarse_kernel, chosen, 4.0 * step_size),
            (kept(inputs),) if last else (kept(inputs), plain((rows, depth), BF16)),
            held_weights, biases, forcing, pair_weight, pair_bias, pair_forcing, got, top,
            scratch=rounded, flops=2 * layer_flops,
        )
        return got, mid, *new_top

    here = lax.axis_index("layer")
    slot, group = here % 4, here // 4
    last_group = groups - 1

    def single(factor, got, added):
        return call(
            functools.partial(single_kernel, factor), plain((rows, depth), F32),
            held_weights, biases, got, added, flops=layer_flops,
        )

    def finish(gots, mids):
        got_1, got_2, got_3 = gots
        mid_1, mid_2, mid_3 = mids
        held = call(held_kernel, plain((rows, depth), BF16), got_1, got_2, got_3)
        down = along(held, down_pair)
        return call(
            functools.partial(final_kernel, step_size),
            (plain((rows, depth), BF16), kept(inputs), plain((rows, depth), F32)),
            held_weights, biases, inputs, start, down, mid_2, mid_1, mid_3, forcing, relaxed,
            scratch=rounded, flops=3 * layer_flops,
        )

    top_0 = ahead
    if groups > 2:
        after = single(4.0 * step_size, along(ahead, up_pair), forcing)
        top_0 = jnp.where((slot == 1) & (group > 0), after.astype(BF16), ahead)
    got_1, mid_1, top_1 = two_steps(
        top_0, [(4 * m + 1, 4 * m + 3) for m in range(groups - 1)], lambda slot, group: (slot == 3) & (group < last_group)
    )
    top_1, *sent_adjoints = lax.optimization_barrier((top_1, *sent_adjoints))
    adjoints = sent_adjoints[:1] + [shifted(sent_adjoints[by], by) for by in range(1, parts)]
    got_2, mid_2, top_2 = two_steps(
        top_1, [(4 * m - 1, 4 * m + 1) for m in range(1, groups)], lambda slot, group: (slot == 1) & (group > 0),
        beside=adjoints,
    )
    got_3, mid_3 = two_steps(
        top_2, [(4 * m + 1, 4 * m + 3) for m in range(1, groups)], lambda slot, group: (slot == 3) & (group > 0), True
    )
    top_last = top_2
    left, state, coarse_states = finish((got_1, got_2, got_3), (mid_1, mid_2, mid_3))
    if groups > 2:
        late = lambda slot, group: group > 1
        relaxed_out = call(functools.partial(pick_kernel, late), plain((rows, depth), F32), relaxed, relaxed)
        solved = coarse_states + relaxed_out
        below = along(top_1, [(4 * m - 1, 4 * m + 3) for m in range(2, groups)])
        base = solved - single(16.0 * step_size, below, jnp.zeros((rows, depth), F32))
        for m in range(2, groups):
            new = single(16.0 * step_size, along(solved.astype(BF16), [(4 * m - 1, 4 * m + 3)]), base)
            solved = jnp.where(here == 4 * m + 3, new, solved)
        new_2, new_mid_2, top_last = two_steps(
            jnp.where(slot == 3, solved.astype(BF16), top_2), [(4 * m - 1, 4 * m + 1) for m in range(2, groups)], lambda slot, group: (slot == 1) & (group > 1)
        )
        new_3, new_mid_3 = two_steps(
            top_last, [(4 * m + 1, 4 * m + 3) for m in range(2, groups)], lambda slot, group: (slot == 3) & (group > 1), True
        )
        mids = [
            call(functools.partial(pick_kernel, late), kept(inputs), new, old)
            for new, old in ((new_mid_2, mid_2), (new_mid_3, mid_3))
        ]
        gots = [jnp.where(group > 1, new, old) for new, old in ((new_2, got_2), (new_3, got_3))]
        left, state, coarse_early = finish((got_1, *gots), (mid_1, *mids))
        coarse_states = jnp.where(slot == 3, solved - relaxed_out, coarse_states)
    far = [across(top_last, [(0, 0)] + [(i, i + 1) for i in range(1, blocks - 1, 2)], by) for by in range(1, parts)]
    odd_lefts = [across(left, [(i, i) for i in range(1, blocks, 2)], by) for by in range(1, parts)]
    new_states = call(
        functools.partial(last_kernel, step_size), plain((rows, depth), F32),
        held_weights, biases, left, state, flops=layer_flops,
    )
    deltas = pltpu.VMEM((rows, width), BF16)
    total = call(
        functools.partial(own_gradient_kernel, step_size), pltpu.VMEM((depth, width), F32),
        held_weights, biases, left, adjoints[0], scratch=[deltas], flops=layer_flops // 2,
    )
    others = (parts - 1) * rows
    total = call(
        functools.partial(even_kernel, step_size, rows, parts - 1), pltpu.VMEM((depth, width), F32),
        held_weights, biases, total, *far, *adjoints[1:],
        scratch=[pltpu.VMEM((others, depth), F32)] + [pltpu.VMEM((others, depth), BF16)] * 2
        + [pltpu.VMEM((others, width), BF16)] * 2,
        flops=4 * (parts - 1) * layer_flops,
    )
    weight_grad = call(
        functools.partial(odd_kernel, step_size, parts - 1), plain((depth, width), F32),
        held_weights, biases, total, *odd_lefts, *adjoints[1:], scratch=[deltas], flops=2 * layer_flops,
    )
    return (new_states[None], coarse_states[None], weight_grad[None])


def solution(mesh):
    return jax.shard_map(
        body,
        mesh=mesh,
        in_specs=(
            P("dp", None),
            P("layer", "dp", None),
            P("layer", None, None),
            P("layer", None),
            P("layer", "dp", None),
        ),
        out_specs=(P("layer", "dp", None), P("layer", "dp", None), P("layer", None, "dp")),
        check_vma=False,
    )
```

```python
import functools

import jax
import jax.numpy as jnp
from jax import lax
from jax.experimental import pallas as pl
from jax.experimental.pallas import tpu as pltpu
from jax.sharding import PartitionSpec as P

BF16 = jnp.bfloat16
F32 = jnp.float32
TILE = 256
EXTRA = 16
WHOLE = pl.BlockSpec(memory_space=pltpu.VMEM)
BULK = pl.BlockSpec(memory_space=pltpu.HBM)


def call(kernel, outs, *args, scratch=(), flops=0, specs=None):
    moved = sum(a.size * a.dtype.itemsize for a in args)
    return pl.pallas_call(
        kernel,
        out_shape=outs,
        in_specs=specs or [WHOLE] * len(args),
        out_specs=jax.tree.map(lambda _: WHOLE, outs, is_leaf=lambda leaf: not isinstance(leaf, (tuple, list))),
        scratch_shapes=list(scratch),
        compiler_params=pltpu.CompilerParams(vmem_limit_bytes=8 << 20),
        cost_estimate=pl.CostEstimate(flops=flops, bytes_accessed=moved, transcendentals=0),
    )(*args)


def kept(like, dtype=None):
    return pltpu.VMEM(like.shape, dtype or like.dtype)


def plain(shape, dtype):
    return jax.ShapeDtypeStruct(shape, dtype)


def tiles(width):
    step = min(TILE, width)
    return [slice(at, at + step) for at in range(0, width, step)]


def layer_of(rounded_ref, weight_ref, bias, cols):
    product = jnp.dot(rounded_ref[...], weight_ref[:, cols], preferred_element_type=F32)
    return jnp.tanh(product + bias[:, cols])


def round_kernel(guess, sent_guess):
    sent_guess[...] = guess[...].astype(BF16)


def columns_kernel(parts, adjoint, *columns):
    width = adjoint.shape[1] // parts
    for by, target in enumerate(columns):
        index = lax.rem(lax.axis_index("dp") + by, parts)
        target[...] = adjoint[:, pl.ds(pl.multiple_of(index * width, width), width)]


def load_kernel(source, target, coarse_weight, sems):
    layers, depth = source.shape[:2]
    pieces = (sems.shape[0] - 1) // layers
    step = depth // pieces
    copies = [
        pltpu.make_async_copy(
            source.at[i, pl.ds(at * step, step)], target.at[i, pl.ds(at * step, step)], sems.at[i * pieces + at]
        )
        for i in range(layers)
        for at in range(pieces)
    ]
    for copy in copies:
        copy.start()
    for copy in copies[:pieces]:
        copy.wait()
    again = pltpu.make_async_copy(target.at[0], coarse_weight, sems.at[layers * pieces])
    again.start()
    for copy in copies[pieces:]:
        copy.wait()
    again.wait()


def run_layers(layers, step_size, weights, biases, state, rounded):
    for layer in layers:
        bias = biases[layer : layer + 1, :]
        now, later = rounded[layer % 2], rounded[(layer + 1) % 2]
        for cols in tiles(state.shape[1]):
            new = state[:, cols] + step_size * layer_of(now, weights.at[layer], bias, cols)
            state[:, cols] = new
            later[:, cols] = new.astype(BF16)


def relax_kernel(step_size, rows, weights, biases, inputs, got, relaxed, sent, even, odd):
    first = lax.axis_index("layer") == 0

    @pl.when(first)
    def _():
        relaxed[...] = inputs[...]

    @pl.when(jnp.logical_not(first))
    def _():
        relaxed[...] = got[...].astype(F32)

    even[...] = relaxed[...].astype(BF16)
    run_layers(range(4), step_size, weights, biases, relaxed, (even, odd))
    sent[:rows, :] = even[...]
    bias = biases[0:1, :]
    high = bias.astype(BF16)
    rest = bias - high.astype(F32)
    middle = rest.astype(BF16)
    low = (rest - middle.astype(F32)).astype(BF16)
    at = lax.broadcasted_iota(jnp.int32, (EXTRA, bias.shape[1]), 0)
    parts = jnp.where(at == 0, high.astype(F32), jnp.where(at == 1, middle.astype(F32), low.astype(F32)))
    sent[rows:, :] = jnp.where(at < 3, parts, 0.0).astype(BF16)


def ahead_kernel(step_size, rows, weights, biases, inputs, got, start, forcing, pair_bias, top, sent_forcing, state, even, odd):
    first = lax.axis_index("layer") == 0

    @pl.when(first)
    def _():
        start[...] = inputs[...]

    @pl.when(jnp.logical_not(first))
    def _():
        start[...] = got[:rows, :].astype(F32)

    even[...] = start[...].astype(BF16)
    bias = biases[0:1, :]
    for cols in tiles(state.shape[1]):
        slope = layer_of(even, weights.at[0], bias, cols)
        new = start[:, cols] + step_size * slope
        state[:, cols] = new
        odd[:, cols] = new.astype(BF16)
        forcing[:, cols] = start[:, cols] + (4.0 * step_size) * slope
    run_layers((1, 2, 3), step_size, weights, biases, state, (even, odd))
    top[...] = jnp.where(first, inputs[...].astype(BF16), even[...])
    difference = state[...] - forcing[...]
    forcing[...] = difference
    sent_forcing[...] = difference.astype(BF16)
    tail = got[rows:, :].astype(F32)
    pair_bias[...] = jnp.broadcast_to(tail[0:1, :] + (tail[1:2, :] + tail[2:3, :]), pair_bias.shape)


def coarse_kernel(chosen, factor, weights, biases, forcing, pair_weight, pair_bias, pair_forcing, got, before, mid, *rest):
    even, odd = rest[-2:]
    here = lax.axis_index("layer")

    taken = chosen(here % 4, here // 4)

    @pl.when(jnp.logical_not(taken))
    def _():
        for top in rest[:-2]:
            top[...] = before[...]

    @pl.when(taken)
    def _():
        even[...] = got[...]
        for cols in tiles(mid.shape[1]):
            slope = layer_of(even, pair_weight, pair_bias[0:1, :], cols)
            new = got[:, cols].astype(F32) + factor * slope + pair_forcing[:, cols].astype(F32)
            mid[:, cols] = new
            odd[:, cols] = new.astype(BF16)
        bias = biases[0:1, :]
        for top in rest[:-2]:
            for cols in tiles(mid.shape[1]):
                slope = layer_of(odd, weights.at[0], bias, cols)
                top[:, cols] = (mid[:, cols] + factor * slope + forcing[:, cols]).astype(BF16)


def final_kernel(step_size, weights, biases, inputs, one, got_first, got_low, got_high, low_mid, first_mid, high_mid, forcing, relaxed, left, state, coarse, even, odd):
    here = lax.axis_index("layer")
    slot, group = here % 4, here // 4

    def start_from(condition, source):
        @pl.when(condition)
        def _():
            state[...] = source[...].astype(F32)

    start_from(here == 0, inputs)
    start_from(here == 1, one)
    start_from((slot == 2) & (group == 0), got_first)
    start_from((slot == 0) & (group > 0), got_low)
    start_from((slot == 2) & (group > 0), got_high)
    start_from((slot == 1) & (group > 0), low_mid)
    start_from((slot == 3) & (group == 0), first_mid)
    start_from((slot == 3) & (group > 0), high_mid)
    even[...] = state[...].astype(BF16)
    bias = biases[0:1, :]
    for cols in tiles(state.shape[1]):
        slope = layer_of(even, weights.at[0], bias, cols)
        old = state[:, cols]
        new = old + step_size * slope
        coarse[:, cols] = old + (4.0 * step_size) * slope + forcing[:, cols] - relaxed[:, cols]
        state[:, cols] = new
        odd[:, cols] = new.astype(BF16)
    run_layers((1, 2), step_size, weights, biases, state, (even, odd))
    left[...] = odd[...]


def last_kernel(step_size, weights, biases, left, state, new_states):
    bias = biases[3:4, :]
    for cols in tiles(state.shape[1]):
        new_states[:, cols] = state[:, cols] + step_size * layer_of(left, weights.at[3], bias, cols)


def gradient(step_size, weights, biases, left, adjoint, deltas, width):
    cols = pl.ds(pl.multiple_of(lax.axis_index("dp") * width, width), width)
    slope = jnp.tanh(jnp.dot(left[...], weights[3, :, cols], preferred_element_type=F32) + biases[3:4, cols])
    deltas[...] = (adjoint[...].astype(F32) * step_size * (1.0 - slope * slope)).astype(BF16)
    return lax.dot_general(left[...], deltas[...], (((0,), (0,)), ((), ())), preferred_element_type=F32)


def own_gradient_kernel(step_size, weights, biases, left, adjoint, total, deltas):
    total[...] = gradient(step_size, weights, biases, left, adjoint, deltas, total.shape[1])


def even_kernel(step_size, rows, count, weights, biases, total, *refs):
    first, low, high, adjoints = (refs[i * count : (i + 1) * count] for i in range(4))
    result, state, even, odd, adjoint, deltas = refs[4 * count :]
    here = lax.axis_index("layer")
    slot, group = here % 4, here // 4
    is_even = here % 2 == 0

    def start_from(condition, sources):
        @pl.when(condition)
        def _():
            for i, source in enumerate(sources):
                even[i * rows : (i + 1) * rows, :] = source[...]

    start_from((here == 0) | ((slot == 2) & (group == 0)), first)
    start_from((slot == 0) & (group > 0), low)
    start_from((slot == 2) & (group > 0), high)

    @pl.when(jnp.logical_not(is_even))
    def _():
        result[...] = total[...]

    @pl.when(is_even)
    def _():
        state[...] = even[...].astype(F32)
        for i, columns in enumerate(adjoints):
            adjoint[i * rows : (i + 1) * rows, :] = columns[...]
        run_layers((0, 1, 2), step_size, weights, biases, state, (even, odd))
        result[...] = total[...] + gradient(step_size, weights, biases, odd, adjoint, deltas, result.shape[1])


def odd_kernel(step_size, count, weights, biases, total, *refs):
    lefts, adjoints = refs[:count], refs[count : 2 * count]
    result, deltas = refs[2 * count :]
    result[...] = total[...]

    @pl.when(lax.axis_index("layer") % 2 == 1)
    def _():
        for left, adjoint in zip(lefts, adjoints):
            result[...] += gradient(step_size, weights, biases, left, adjoint, deltas, result.shape[1])


def single_kernel(factor, weights, biases, got, added, out):
    for cols in tiles(out.shape[1]):
        slope = layer_of(got, weights.at[0], biases[0:1, :], cols)
        out[:, cols] = got[:, cols].astype(F32) + factor * slope + added[:, cols]


def pick_kernel(chosen, new, old, out):
    here = lax.axis_index("layer")
    out[...] = jnp.where(chosen(here % 4, here // 4), new[...], old[...])


def body(inputs, guesses, weights, biases, adjoint):
    blocks = lax.axis_size("layer")
    parts = lax.axis_size("dp")
    groups = blocks // 4
    step_size = 4.0 / (4 * blocks)
    rows, depth = inputs.shape
    width = depth // parts
    layer_flops = 2 * rows * depth * depth

    def along(state, pairs):
        return lax.ppermute(state, "layer", pairs)

    def across(state, pairs, by):
        flat = [(i * parts + z, j * parts + (z + by) % parts) for i, j in pairs for z in range(parts) if by or i != j]
        return lax.ppermute(state, ("layer", "dp"), flat)

    def shifted(array, by):
        return lax.ppermute(array, "dp", [(i, (i + by) % parts) for i in range(parts)])

    up = [(i, i + 1) for i in range(blocks - 1)]
    up_pair = [(i, i + 1) for i in range(0, blocks, 2)]
    rounded = [pltpu.VMEM((rows, depth), BF16)] * 2

    guess_sent = call(round_kernel, plain((rows, depth), BF16), guesses[0])
    guess_prev = along(guess_sent, up)
    guess_sent, weights = lax.optimization_barrier((guess_sent, weights))
    held_weights, coarse_weight = call(
        load_kernel, (kept(weights), plain((depth, depth), BF16)), pltpu.with_memory_space_constraint(weights, pltpu.HBM),
        scratch=[pltpu.SemaphoreType.DMA((weights.shape[0] * 4 + 1,))], specs=[BULK],
    )
    guess_prev, coarse_weight = lax.optimization_barrier((guess_prev, coarse_weight))
    pair_weight = along(coarse_weight, up_pair)
    sent_adjoints = call(
        functools.partial(columns_kernel, parts), (plain((rows, width), BF16),) * parts, adjoint[0]
    )
    relaxed, relaxed_sent = call(
        functools.partial(relax_kernel, step_size, rows),
        (kept(inputs), plain((rows + EXTRA, depth), BF16)),
        held_weights, biases, inputs, guess_prev,
        scratch=rounded, flops=4 * layer_flops,
    )
    relaxed_got = along(relaxed_sent, up)
    start, forcing, pair_bias, ahead, forcing_sent = call(
        functools.partial(ahead_kernel, step_size, rows),
        (kept(inputs), kept(inputs), pltpu.VMEM((8, depth), F32), plain((rows, depth), BF16), plain((rows, depth), BF16)),
        held_weights, biases, inputs, relaxed_got,
        scratch=[pltpu.VMEM((rows, depth), F32)] + rounded, flops=4 * layer_flops,
    )
    pair_forcing = along(forcing_sent, up_pair)

    def two_steps(top, pairs, chosen, last=False, beside=()):
        got, *_ = lax.optimization_barrier((along(top, pairs), *beside))
        mid, *new_top = call(
            functools.partial(coarse_kernel, chosen, 4.0 * step_size),
            (kept(inputs),) if last else (kept(inputs), plain((rows, depth), BF16)),
            held_weights, biases, forcing, pair_weight, pair_bias, pair_forcing, got, top,
            scratch=rounded, flops=2 * layer_flops,
        )
        return got, mid, *new_top

    here = lax.axis_index("layer")
    slot, group = here % 4, here // 4
    last_group = groups - 1

    def single(factor, got, added):
        return call(
            functools.partial(single_kernel, factor), plain((rows, depth), F32),
            held_weights, biases, got, added, flops=layer_flops,
        )

    def finish(even_starts, mids):
        mid_1, mid_2, mid_3 = mids
        return call(
            functools.partial(final_kernel, step_size),
            (plain((rows, depth), BF16), kept(inputs), plain((rows, depth), F32)),
            held_weights, biases, inputs, start, *even_starts, mid_2, mid_1, mid_3, forcing, relaxed,
            scratch=rounded, flops=3 * layer_flops,
        )

    def to_planes(state, pairs):
        return [across(state, pairs, by) for by in range(parts)]

    top_0 = ahead
    if groups > 2:
        after = single(4.0 * step_size, along(ahead, up_pair), forcing)
        top_0 = jnp.where((slot == 1) & (group > 0), after.astype(BF16), ahead)
    _, mid_1, top_1 = two_steps(
        top_0, [(4 * m + 1, 4 * m + 3) for m in range(groups - 1)], lambda slot, group: (slot == 3) & (group < last_group)
    )
    far_1 = to_planes(top_0, [(0, 0)] + [(4 * m + 1, 4 * m + 2) for m in range(1)])
    top_1, *sent_adjoints = lax.optimization_barrier((top_1, *sent_adjoints))
    adjoints = sent_adjoints[:1] + [shifted(sent_adjoints[by], by) for by in range(1, parts)]
    _, mid_2, top_2 = two_steps(
        top_1, [(4 * m - 1, 4 * m + 1) for m in range(1, groups)], lambda slot, group: (slot == 1) & (group > 0),
        beside=(*adjoints, *far_1),
    )
    far_2 = to_planes(top_1, [(4 * m - 1, 4 * m) for m in range(1, groups)])
    _, mid_3 = two_steps(
        top_2, [(4 * m + 1, 4 * m + 3) for m in range(1, groups)], lambda slot, group: (slot == 3) & (group > 0), True,
        beside=far_2,
    )
    far_3 = to_planes(top_2, [(4 * m + 1, 4 * m + 2) for m in range(1, groups)])
    left, state, coarse_states = finish((far_1[0], far_2[0], far_3[0]), (mid_1, mid_2, mid_3))
    if groups > 2:
        late = lambda slot, group: group > 1
        relaxed_out = call(functools.partial(pick_kernel, late), plain((rows, depth), F32), relaxed, relaxed)
        solved = coarse_states + relaxed_out
        below = along(top_1, [(4 * m - 1, 4 * m + 3) for m in range(2, groups)])
        base = solved - single(16.0 * step_size, below, jnp.zeros((rows, depth), F32))
        for m in range(2, groups):
            new = single(16.0 * step_size, along(solved.astype(BF16), [(4 * m - 1, 4 * m + 3)]), base)
            solved = jnp.where(here == 4 * m + 3, new, solved)
        _, new_mid_2, top_2 = two_steps(
            solved.astype(BF16), [(4 * m - 1, 4 * m + 1) for m in range(2, groups)], lambda slot, group: (slot == 1) & (group > 1)
        )
        _, new_mid_3 = two_steps(
            top_2, [(4 * m + 1, 4 * m + 3) for m in range(2, groups)], lambda slot, group: (slot == 3) & (group > 1), True
        )
        new_far_2 = to_planes(solved.astype(BF16), [(4 * m - 1, 4 * m) for m in range(2, groups)])
        new_far_3 = to_planes(top_2, [(4 * m + 1, 4 * m + 2) for m in range(2, groups)])
        picked = functools.partial(pick_kernel, late)
        mids = [call(picked, kept(inputs), new, old) for new, old in ((new_mid_2, mid_2), (new_mid_3, mid_3))]
        far_2, far_3 = (
            [call(picked, plain((rows, depth), BF16), new, old) for new, old in zip(*pair)]
            for pair in ((new_far_2, far_2), (new_far_3, far_3))
        )
        left, state, _ = finish((far_1[0], far_2[0], far_3[0]), (mid_1, *mids))
        coarse_states = jnp.where(slot == 3, solved - relaxed_out, coarse_states)
    odd_lefts = [across(left, [(i, i) for i in range(1, blocks, 2)], by) for by in range(1, parts)]
    new_states = call(
        functools.partial(last_kernel, step_size), plain((rows, depth), F32),
        held_weights, biases, left, state, flops=layer_flops,
    )
    deltas = pltpu.VMEM((rows, width), BF16)
    total = call(
        functools.partial(own_gradient_kernel, step_size), pltpu.VMEM((depth, width), F32),
        held_weights, biases, left, adjoints[0], scratch=[deltas], flops=layer_flops // 2,
    )
    others = (parts - 1) * rows
    total = call(
        functools.partial(even_kernel, step_size, rows, parts - 1), pltpu.VMEM((depth, width), F32),
        held_weights, biases, total, *far_1[1:], *far_2[1:], *far_3[1:], *adjoints[1:],
        scratch=[pltpu.VMEM((others, depth), F32)] + [pltpu.VMEM((others, depth), BF16)] * 2
        + [pltpu.VMEM((others, width), BF16)] * 2,
        flops=4 * (parts - 1) * layer_flops,
    )
    weight_grad = call(
        functools.partial(odd_kernel, step_size, parts - 1), plain((depth, width), F32),
        held_weights, biases, total, *odd_lefts, *adjoints[1:], scratch=[deltas], flops=2 * layer_flops,
    )
    return (new_states[None], coarse_states[None], weight_grad[None])


def solution(mesh):
    return jax.shard_map(
        body,
        mesh=mesh,
        in_specs=(
            P("dp", None),
            P("layer", "dp", None),
            P("layer", None, None),
            P("layer", None),
            P("layer", "dp", None),
        ),
        out_specs=(P("layer", "dp", None), P("layer", "dp", None), P("layer", None, "dp")),
        check_vma=False,
    )
```

```python
import functools

import jax
import jax.numpy as jnp
from jax import lax
from jax.experimental import pallas as pl
from jax.experimental.pallas import tpu as pltpu
from jax.sharding import PartitionSpec as P

BF16 = jnp.bfloat16
F32 = jnp.float32
TILE = 256
EXTRA = 16
WHOLE = pl.BlockSpec(memory_space=pltpu.VMEM)
BULK = pl.BlockSpec(memory_space=pltpu.HBM)


def call(kernel, outs, *args, scratch=(), flops=0, specs=None):
    moved = sum(a.size * a.dtype.itemsize for a in args)
    return pl.pallas_call(
        kernel,
        out_shape=outs,
        in_specs=specs or [WHOLE] * len(args),
        out_specs=jax.tree.map(lambda _: WHOLE, outs, is_leaf=lambda leaf: not isinstance(leaf, (tuple, list))),
        scratch_shapes=list(scratch),
        compiler_params=pltpu.CompilerParams(vmem_limit_bytes=8 << 20),
        cost_estimate=pl.CostEstimate(flops=flops, bytes_accessed=moved, transcendentals=0),
    )(*args)


def kept(like, dtype=None):
    return pltpu.VMEM(like.shape, dtype or like.dtype)


def plain(shape, dtype):
    return jax.ShapeDtypeStruct(shape, dtype)


def tiles(width):
    step = min(TILE, width)
    return [slice(at, at + step) for at in range(0, width, step)]


def layer_of(rounded_ref, weight_ref, bias, cols):
    product = jnp.dot(rounded_ref[...], weight_ref[:, cols], preferred_element_type=F32)
    return jnp.tanh(product + bias[:, cols])


def round_kernel(guess, inputs, sent_guess, sent_inputs):
    sent_guess[...] = guess[...].astype(BF16)
    sent_inputs[...] = inputs[...].astype(BF16)


def columns_kernel(parts, adjoint, *columns):
    width = adjoint.shape[1] // parts
    for by, target in enumerate(columns):
        index = lax.rem(lax.axis_index("dp") + by, parts)
        target[...] = adjoint[:, pl.ds(pl.multiple_of(index * width, width), width)]


def load_kernel(source, target, coarse_weight, sems):
    layers, depth = source.shape[:2]
    pieces = (sems.shape[0] - 1) // layers
    step = depth // pieces
    copies = [
        pltpu.make_async_copy(
            source.at[i, pl.ds(at * step, step)], target.at[i, pl.ds(at * step, step)], sems.at[i * pieces + at]
        )
        for i in range(layers)
        for at in range(pieces)
    ]
    for copy in copies:
        copy.start()
    for copy in copies[:pieces]:
        copy.wait()
    again = pltpu.make_async_copy(target.at[0], coarse_weight, sems.at[layers * pieces])
    again.start()
    for copy in copies[pieces:]:
        copy.wait()
    again.wait()


def run_layers(layers, step_size, weights, biases, state, rounded):
    for layer in layers:
        bias = biases[layer : layer + 1, :]
        now, later = rounded[layer % 2], rounded[(layer + 1) % 2]
        for cols in tiles(state.shape[1]):
            new = state[:, cols] + step_size * layer_of(now, weights.at[layer], bias, cols)
            state[:, cols] = new
            later[:, cols] = new.astype(BF16)


def relax_kernel(step_size, rows, weights, biases, inputs, got, relaxed, sent, even, odd):
    first = lax.axis_index("layer") == 0

    @pl.when(first)
    def _():
        relaxed[...] = inputs[...]

    @pl.when(jnp.logical_not(first))
    def _():
        relaxed[...] = got[...].astype(F32)

    even[...] = relaxed[...].astype(BF16)
    run_layers(range(4), step_size, weights, biases, relaxed, (even, odd))
    sent[:rows, :] = even[...]
    bias = biases[0:1, :]
    high = bias.astype(BF16)
    rest = bias - high.astype(F32)
    middle = rest.astype(BF16)
    low = (rest - middle.astype(F32)).astype(BF16)
    at = lax.broadcasted_iota(jnp.int32, (EXTRA, bias.shape[1]), 0)
    parts = jnp.where(at == 0, high.astype(F32), jnp.where(at == 1, middle.astype(F32), low.astype(F32)))
    sent[rows:, :] = jnp.where(at < 3, parts, 0.0).astype(BF16)


def ahead_kernel(step_size, rows, weights, biases, inputs, got, start, forcing, pair_bias, top, sent_forcing, state, even, odd):
    first = lax.axis_index("layer") == 0

    @pl.when(first)
    def _():
        start[...] = inputs[...]

    @pl.when(jnp.logical_not(first))
    def _():
        start[...] = got[:rows, :].astype(F32)

    even[...] = start[...].astype(BF16)
    bias = biases[0:1, :]
    for cols in tiles(state.shape[1]):
        slope = layer_of(even, weights.at[0], bias, cols)
        new = start[:, cols] + step_size * slope
        state[:, cols] = new
        odd[:, cols] = new.astype(BF16)
        forcing[:, cols] = start[:, cols] + (4.0 * step_size) * slope
    run_layers((1, 2, 3), step_size, weights, biases, state, (even, odd))
    top[...] = even[...]
    difference = state[...] - forcing[...]
    forcing[...] = difference
    sent_forcing[...] = difference.astype(BF16)
    tail = got[rows:, :].astype(F32)
    pair_bias[...] = jnp.broadcast_to(tail[0:1, :] + (tail[1:2, :] + tail[2:3, :]), pair_bias.shape)


def coarse_kernel(chosen, factor, weights, biases, forcing, pair_weight, pair_bias, pair_forcing, got, before, mid, *rest):
    even, odd = rest[-2:]
    here = lax.axis_index("layer")

    taken = chosen(here % 4, here // 4)

    @pl.when(jnp.logical_not(taken))
    def _():
        for top in rest[:-2]:
            top[...] = before[...]

    @pl.when(taken)
    def _():
        even[...] = got[...]
        for cols in tiles(mid.shape[1]):
            slope = layer_of(even, pair_weight, pair_bias[0:1, :], cols)
            new = got[:, cols].astype(F32) + factor * slope + pair_forcing[:, cols].astype(F32)
            mid[:, cols] = new
            odd[:, cols] = new.astype(BF16)
        bias = biases[0:1, :]
        for top in rest[:-2]:
            for cols in tiles(mid.shape[1]):
                slope = layer_of(odd, weights.at[0], bias, cols)
                top[:, cols] = (mid[:, cols] + factor * slope + forcing[:, cols]).astype(BF16)


def held_kernel(got_1, got_2, got_3, held):
    here = lax.axis_index("layer")
    low, early = here % 4 < 2, here // 4 == 0
    held[...] = jnp.where(low, got_2[...], jnp.where(early, got_1[...], got_3[...]))


def final_kernel(step_size, weights, biases, inputs, one, down, low_mid, first_mid, high_mid, forcing, relaxed, left, state, coarse, even, odd):
    here = lax.axis_index("layer")
    slot, group = here % 4, here // 4

    def start_from(condition, source):
        @pl.when(condition)
        def _():
            state[...] = source[...].astype(F32)

    start_from(here == 0, inputs)
    start_from(here == 1, one)
    start_from((here > 0) & (here % 2 == 0), down)
    start_from((slot == 1) & (group > 0), low_mid)
    start_from((slot == 3) & (group == 0), first_mid)
    start_from((slot == 3) & (group > 0), high_mid)
    even[...] = state[...].astype(BF16)
    bias = biases[0:1, :]
    for cols in tiles(state.shape[1]):
        slope = layer_of(even, weights.at[0], bias, cols)
        old = state[:, cols]
        new = old + step_size * slope
        coarse[:, cols] = old + (4.0 * step_size) * slope + forcing[:, cols] - relaxed[:, cols]
        state[:, cols] = new
        odd[:, cols] = new.astype(BF16)
    run_layers((1, 2), step_size, weights, biases, state, (even, odd))
    left[...] = odd[...]


def last_kernel(step_size, weights, biases, left, state, new_states):
    bias = biases[3:4, :]
    for cols in tiles(state.shape[1]):
        new_states[:, cols] = state[:, cols] + step_size * layer_of(left, weights.at[3], bias, cols)


def gradient(step_size, weights, biases, left, adjoint, deltas, width):
    cols = pl.ds(pl.multiple_of(lax.axis_index("dp") * width, width), width)
    slope = jnp.tanh(jnp.dot(left[...], weights[3, :, cols], preferred_element_type=F32) + biases[3:4, cols])
    deltas[...] = (adjoint[...].astype(F32) * step_size * (1.0 - slope * slope)).astype(BF16)
    return lax.dot_general(left[...], deltas[...], (((0,), (0,)), ((), ())), preferred_element_type=F32)


def own_gradient_kernel(step_size, weights, biases, left, adjoint, total, deltas):
    total[...] = gradient(step_size, weights, biases, left, adjoint, deltas, total.shape[1])


def even_kernel(step_size, rows, count, weights, biases, total, *refs):
    points, starts, adjoints = (refs[i * count : (i + 1) * count] for i in range(3))
    result, state, even, odd, adjoint, deltas = refs[3 * count :]
    here = lax.axis_index("layer")
    is_even = here % 2 == 0

    def start_from(condition, sources):
        @pl.when(condition)
        def _():
            for i, source in enumerate(sources):
                even[i * rows : (i + 1) * rows, :] = source[...]

    start_from(here == 0, points)
    start_from((here > 0) & is_even, starts)

    @pl.when(jnp.logical_not(is_even))
    def _():
        result[...] = total[...]

    @pl.when(is_even)
    def _():
        state[...] = even[...].astype(F32)
        for i, columns in enumerate(adjoints):
            adjoint[i * rows : (i + 1) * rows, :] = columns[...]
        run_layers((0, 1, 2), step_size, weights, biases, state, (even, odd))
        result[...] = total[...] + gradient(step_size, weights, biases, odd, adjoint, deltas, result.shape[1])


def odd_kernel(step_size, count, weights, biases, total, *refs):
    lefts, adjoints = refs[:count], refs[count : 2 * count]
    result, deltas = refs[2 * count :]
    result[...] = total[...]

    @pl.when(lax.axis_index("layer") % 2 == 1)
    def _():
        for left, adjoint in zip(lefts, adjoints):
            result[...] += gradient(step_size, weights, biases, left, adjoint, deltas, result.shape[1])


def single_kernel(factor, weights, biases, got, added, out):
    for cols in tiles(out.shape[1]):
        slope = layer_of(got, weights.at[0], biases[0:1, :], cols)
        out[:, cols] = got[:, cols].astype(F32) + factor * slope + added[:, cols]


def pick_kernel(chosen, new, old, out):
    here = lax.axis_index("layer")
    out[...] = jnp.where(chosen(here % 4, here // 4), new[...], old[...])


def body(inputs, guesses, weights, biases, adjoint):
    blocks = lax.axis_size("layer")
    parts = lax.axis_size("dp")
    groups = blocks // 4
    step_size = 4.0 / (4 * blocks)
    rows, depth = inputs.shape
    width = depth // parts
    layer_flops = 2 * rows * depth * depth

    def along(state, pairs):
        return lax.ppermute(state, "layer", pairs)

    def across(state, pairs, by):
        flat = [(i * parts + z, j * parts + (z + by) % parts) for i, j in pairs for z in range(parts)]
        return lax.ppermute(state, ("layer", "dp"), flat)

    def shifted(array, by):
        return lax.ppermute(array, "dp", [(i, (i + by) % parts) for i in range(parts)])

    up = [(i, i + 1) for i in range(blocks - 1)]
    up_pair = [(i, i + 1) for i in range(0, blocks, 2)]
    down_pair = [(i + 1, i) for i in range(0, blocks, 2)]
    rounded = [pltpu.VMEM((rows, depth), BF16)] * 2

    guess_sent, inputs_sent = call(round_kernel, (plain((rows, depth), BF16),) * 2, guesses[0], inputs)
    guess_prev = along(guess_sent, up)
    guess_sent, weights = lax.optimization_barrier((guess_sent, weights))
    held_weights, coarse_weight = call(
        load_kernel, (kept(weights), plain((depth, depth), BF16)), pltpu.with_memory_space_constraint(weights, pltpu.HBM),
        scratch=[pltpu.SemaphoreType.DMA((weights.shape[0] * 4 + 1,))], specs=[BULK],
    )
    guess_prev, coarse_weight = lax.optimization_barrier((guess_prev, coarse_weight))
    pair_weight = along(coarse_weight, up_pair)
    sent_adjoints = call(
        functools.partial(columns_kernel, parts), (plain((rows, width), BF16),) * parts, adjoint[0]
    )
    relaxed, relaxed_sent = call(
        functools.partial(relax_kernel, step_size, rows),
        (kept(inputs), plain((rows + EXTRA, depth), BF16)),
        held_weights, biases, inputs, guess_prev,
        scratch=rounded, flops=4 * layer_flops,
    )
    relaxed_sent, inputs_sent = lax.optimization_barrier((relaxed_sent, inputs_sent))
    relaxed_got = along(relaxed_sent, up)
    far_inputs = [across(inputs_sent, [(0, 0)], by) for by in range(1, parts)]
    relaxed_got, *far_inputs = lax.optimization_barrier((relaxed_got, *far_inputs))
    start, forcing, pair_bias, ahead, forcing_sent = call(
        functools.partial(ahead_kernel, step_size, rows),
        (kept(inputs), kept(inputs), pltpu.VMEM((8, depth), F32), plain((rows, depth), BF16), plain((rows, depth), BF16)),
        held_weights, biases, inputs, relaxed_got,
        scratch=[pltpu.VMEM((rows, depth), F32)] + rounded, flops=4 * layer_flops,
    )
    pair_forcing = along(forcing_sent, up_pair)

    def two_steps(top, pairs, chosen, last=False, beside=()):
        got, *_ = lax.optimization_barrier((along(top, pairs), *beside))
        mid, *new_top = call(
            functools.partial(coarse_kernel, chosen, 4.0 * step_size),
            (kept(inputs),) if last else (kept(inputs), plain((rows, depth), BF16)),
            held_weights, biases, forcing, pair_weight, pair_bias, pair_forcing, got, top,
            scratch=rounded, flops=2 * layer_flops,
        )
        return got, mid, *new_top

    here = lax.axis_index("layer")
    slot, group = here % 4, here // 4
    last_group = groups - 1

    def single(factor, got, added):
        return call(
            functools.partial(single_kernel, factor), plain((rows, depth), F32),
            held_weights, biases, got, added, flops=layer_flops,
        )

    def finish(gots, mids):
        got_1, got_2, got_3 = gots
        mid_1, mid_2, mid_3 = mids
        held = call(held_kernel, plain((rows, depth), BF16), got_1, got_2, got_3)
        down = along(held, down_pair)
        return call(
            functools.partial(final_kernel, step_size),
            (plain((rows, depth), BF16), kept(inputs), plain((rows, depth), F32)),
            held_weights, biases, inputs, start, down, mid_2, mid_1, mid_3, forcing, relaxed,
            scratch=rounded, flops=3 * layer_flops,
        )

    top_0 = ahead
    if groups > 2:
        after = single(4.0 * step_size, along(ahead, up_pair), forcing)
        top_0 = jnp.where((slot == 1) & (group > 0), after.astype(BF16), ahead)
    got_1, mid_1, top_1 = two_steps(
        top_0, [(4 * m + 1, 4 * m + 3) for m in range(groups - 1)], lambda slot, group: (slot == 3) & (group < last_group)
    )
    top_1, *sent_adjoints = lax.optimization_barrier((top_1, *sent_adjoints))
    adjoints = sent_adjoints[:1] + [shifted(sent_adjoints[by], by) for by in range(1, parts)]
    got_2, mid_2, top_2 = two_steps(
        top_1, [(4 * m - 1, 4 * m + 1) for m in range(1, groups)], lambda slot, group: (slot == 1) & (group > 0),
        beside=adjoints,
    )
    got_3, mid_3 = two_steps(
        top_2, [(4 * m + 1, 4 * m + 3) for m in range(1, groups)], lambda slot, group: (slot == 3) & (group > 0), True
    )
    top_last = top_2
    left, state, coarse_states = finish((got_1, got_2, got_3), (mid_1, mid_2, mid_3))
    if groups > 2:
        late = lambda slot, group: group > 1
        relaxed_out = call(functools.partial(pick_kernel, late), plain((rows, depth), F32), relaxed, relaxed)
        solved = coarse_states + relaxed_out
        below = along(top_1, [(4 * m - 1, 4 * m + 3) for m in range(2, groups)])
        base = solved - single(16.0 * step_size, below, jnp.zeros((rows, depth), F32))
        for m in range(2, groups):
            new = single(16.0 * step_size, along(solved.astype(BF16), [(4 * m - 1, 4 * m + 3)]), base)
            solved = jnp.where(here == 4 * m + 3, new, solved)
        new_2, new_mid_2, top_last = two_steps(
            jnp.where(slot == 3, solved.astype(BF16), top_2), [(4 * m - 1, 4 * m + 1) for m in range(2, groups)], lambda slot, group: (slot == 1) & (group > 1)
        )
        new_3, new_mid_3 = two_steps(
            top_last, [(4 * m + 1, 4 * m + 3) for m in range(2, groups)], lambda slot, group: (slot == 3) & (group > 1), True
        )
        mids = [
            call(functools.partial(pick_kernel, late), kept(inputs), new, old)
            for new, old in ((new_mid_2, mid_2), (new_mid_3, mid_3))
        ]
        gots = [jnp.where(group > 1, new, old) for new, old in ((new_2, got_2), (new_3, got_3))]
        left, state, coarse_early = finish((got_1, *gots), (mid_1, *mids))
        coarse_states = jnp.where(slot == 3, solved - relaxed_out, coarse_states)
    far = [across(top_last, [(i, i + 1) for i in range(1, blocks - 1, 2)], by) for by in range(1, parts)]
    odd_lefts = [across(left, [(i, i) for i in range(1, blocks, 2)], by) for by in range(1, parts)]
    new_states = call(
        functools.partial(last_kernel, step_size), plain((rows, depth), F32),
        held_weights, biases, left, state, flops=layer_flops,
    )
    deltas = pltpu.VMEM((rows, width), BF16)
    total = call(
        functools.partial(own_gradient_kernel, step_size), pltpu.VMEM((depth, width), F32),
        held_weights, biases, left, adjoints[0], scratch=[deltas], flops=layer_flops // 2,
    )
    others = (parts - 1) * rows
    total = call(
        functools.partial(even_kernel, step_size, rows, parts - 1), pltpu.VMEM((depth, width), F32),
        held_weights, biases, total, *far_inputs, *far, *adjoints[1:],
        scratch=[pltpu.VMEM((others, depth), F32)] + [pltpu.VMEM((others, depth), BF16)] * 2
        + [pltpu.VMEM((others, width), BF16)] * 2,
        flops=4 * (parts - 1) * layer_flops,
    )
    weight_grad = call(
        functools.partial(odd_kernel, step_size, parts - 1), plain((depth, width), F32),
        held_weights, biases, total, *odd_lefts, *adjoints[1:], scratch=[deltas], flops=2 * layer_flops,
    )
    return (new_states[None], coarse_states[None], weight_grad[None])


def solution(mesh):
    return jax.shard_map(
        body,
        mesh=mesh,
        in_specs=(
            P("dp", None),
            P("layer", "dp", None),
            P("layer", None, None),
            P("layer", None),
            P("layer", "dp", None),
        ),
        out_specs=(P("layer", "dp", None), P("layer", "dp", None), P("layer", None, "dp")),
        check_vma=False,
    )
```

```python
import functools

import jax
import jax.numpy as jnp
from jax import lax
from jax.experimental import pallas as pl
from jax.experimental.pallas import tpu as pltpu
from jax.sharding import PartitionSpec as P

BF16 = jnp.bfloat16
F32 = jnp.float32
TILE = 256
EXTRA = 16
WHOLE = pl.BlockSpec(memory_space=pltpu.VMEM)
BULK = pl.BlockSpec(memory_space=pltpu.HBM)


def call(kernel, outs, *args, scratch=(), flops=0, specs=None):
    moved = sum(a.size * a.dtype.itemsize for a in args)
    return pl.pallas_call(
        kernel,
        out_shape=outs,
        in_specs=specs or [WHOLE] * len(args),
        out_specs=jax.tree.map(lambda _: WHOLE, outs, is_leaf=lambda leaf: not isinstance(leaf, (tuple, list))),
        scratch_shapes=list(scratch),
        compiler_params=pltpu.CompilerParams(vmem_limit_bytes=8 << 20),
        cost_estimate=pl.CostEstimate(flops=flops, bytes_accessed=moved, transcendentals=0),
    )(*args)


def kept(like, dtype=None):
    return pltpu.VMEM(like.shape, dtype or like.dtype)


def plain(shape, dtype):
    return jax.ShapeDtypeStruct(shape, dtype)


def tiles(width):
    step = min(TILE, width)
    return [slice(at, at + step) for at in range(0, width, step)]


def layer_of(rounded_ref, weight_ref, bias, cols):
    product = jnp.dot(rounded_ref[...], weight_ref[:, cols], preferred_element_type=F32)
    return jnp.tanh(product + bias[:, cols])


def round_kernel(guess, inputs, sent_guess, sent_inputs):
    sent_guess[...] = guess[...].astype(BF16)
    sent_inputs[...] = inputs[...].astype(BF16)


def columns_kernel(parts, adjoint, *columns):
    width = adjoint.shape[1] // parts
    for by, target in enumerate(columns):
        index = lax.rem(lax.axis_index("dp") + by, parts)
        target[...] = adjoint[:, pl.ds(pl.multiple_of(index * width, width), width)]


def load_kernel(source, target, coarse_weight, sems):
    layers, depth = source.shape[:2]
    pieces = (sems.shape[0] - 1) // layers
    step = depth // pieces
    copies = [
        pltpu.make_async_copy(
            source.at[i, pl.ds(at * step, step)], target.at[i, pl.ds(at * step, step)], sems.at[i * pieces + at]
        )
        for i in range(layers)
        for at in range(pieces)
    ]
    for copy in copies:
        copy.start()
    for copy in copies[:pieces]:
        copy.wait()
    again = pltpu.make_async_copy(target.at[0], coarse_weight, sems.at[layers * pieces])
    again.start()
    for copy in copies[pieces:]:
        copy.wait()
    again.wait()


def run_layers(layers, step_size, weights, biases, state, rounded):
    for layer in layers:
        bias = biases[layer : layer + 1, :]
        now, later = rounded[layer % 2], rounded[(layer + 1) % 2]
        for cols in tiles(state.shape[1]):
            new = state[:, cols] + step_size * layer_of(now, weights.at[layer], bias, cols)
            state[:, cols] = new
            later[:, cols] = new.astype(BF16)


def relax_kernel(step_size, rows, weights, biases, inputs, got, relaxed, sent, even, odd):
    first = lax.axis_index("layer") == 0

    @pl.when(first)
    def _():
        relaxed[...] = inputs[...]

    @pl.when(jnp.logical_not(first))
    def _():
        relaxed[...] = got[...].astype(F32)

    even[...] = relaxed[...].astype(BF16)
    run_layers(range(4), step_size, weights, biases, relaxed, (even, odd))
    sent[:rows, :] = even[...]
    bias = biases[0:1, :]
    high = bias.astype(BF16)
    rest = bias - high.astype(F32)
    middle = rest.astype(BF16)
    low = (rest - middle.astype(F32)).astype(BF16)
    at = lax.broadcasted_iota(jnp.int32, (EXTRA, bias.shape[1]), 0)
    parts = jnp.where(at == 0, high.astype(F32), jnp.where(at == 1, middle.astype(F32), low.astype(F32)))
    sent[rows:, :] = jnp.where(at < 3, parts, 0.0).astype(BF16)


def ahead_kernel(step_size, rows, weights, biases, inputs, got, start, forcing, pair_bias, top, sent_forcing, state, even, odd):
    first = lax.axis_index("layer") == 0

    @pl.when(first)
    def _():
        start[...] = inputs[...]

    @pl.when(jnp.logical_not(first))
    def _():
        start[...] = got[:rows, :].astype(F32)

    even[...] = start[...].astype(BF16)
    bias = biases[0:1, :]
    for cols in tiles(state.shape[1]):
        slope = layer_of(even, weights.at[0], bias, cols)
        new = start[:, cols] + step_size * slope
        state[:, cols] = new
        odd[:, cols] = new.astype(BF16)
        forcing[:, cols] = start[:, cols] + (4.0 * step_size) * slope
    run_layers((1, 2, 3), step_size, weights, biases, state, (even, odd))
    top[...] = even[...]
    difference = state[...] - forcing[...]
    forcing[...] = difference
    sent_forcing[...] = difference.astype(BF16)
    tail = got[rows:, :].astype(F32)
    pair_bias[...] = jnp.broadcast_to(tail[0:1, :] + (tail[1:2, :] + tail[2:3, :]), pair_bias.shape)


def coarse_kernel(chosen, factor, weights, biases, forcing, pair_weight, pair_bias, pair_forcing, got, before, mid, *rest):
    even, odd = rest[-2:]
    here = lax.axis_index("layer")

    taken = chosen(here % 4, here // 4)

    @pl.when(jnp.logical_not(taken))
    def _():
        for top in rest[:-2]:
            top[...] = before[...]

    @pl.when(taken)
    def _():
        even[...] = got[...]
        for cols in tiles(mid.shape[1]):
            slope = layer_of(even, pair_weight, pair_bias[0:1, :], cols)
            new = got[:, cols].astype(F32) + factor * slope + pair_forcing[:, cols].astype(F32)
            mid[:, cols] = new
            odd[:, cols] = new.astype(BF16)
        bias = biases[0:1, :]
        for top in rest[:-2]:
            for cols in tiles(mid.shape[1]):
                slope = layer_of(odd, weights.at[0], bias, cols)
                top[:, cols] = (mid[:, cols] + factor * slope + forcing[:, cols]).astype(BF16)


def held_kernel(got_1, got_2, got_3, held):
    here = lax.axis_index("layer")
    low, early = here % 4 < 2, here // 4 == 0
    held[...] = jnp.where(low, got_2[...], jnp.where(early, got_1[...], got_3[...]))


def final_kernel(step_size, weights, biases, inputs, one, down, low_mid, first_mid, high_mid, forcing, relaxed, left, state, coarse, even, odd):
    here = lax.axis_index("layer")
    slot, group = here % 4, here // 4

    def start_from(condition, source):
        @pl.when(condition)
        def _():
            state[...] = source[...].astype(F32)

    start_from(here == 0, inputs)
    start_from(here == 1, one)
    start_from((here > 0) & (here % 2 == 0), down)
    start_from((slot == 1) & (group > 0), low_mid)
    start_from((slot == 3) & (group == 0), first_mid)
    start_from((slot == 3) & (group > 0), high_mid)
    even[...] = state[...].astype(BF16)
    bias = biases[0:1, :]
    for cols in tiles(state.shape[1]):
        slope = layer_of(even, weights.at[0], bias, cols)
        old = state[:, cols]
        new = old + step_size * slope
        coarse[:, cols] = old + (4.0 * step_size) * slope + forcing[:, cols] - relaxed[:, cols]
        state[:, cols] = new
        odd[:, cols] = new.astype(BF16)
    run_layers((1, 2), step_size, weights, biases, state, (even, odd))
    left[...] = odd[...]


def last_kernel(step_size, weights, biases, left, state, new_states):
    bias = biases[3:4, :]
    for cols in tiles(state.shape[1]):
        new_states[:, cols] = state[:, cols] + step_size * layer_of(left, weights.at[3], bias, cols)


def gradient(step_size, weights, biases, left, adjoint, deltas, width):
    cols = pl.ds(pl.multiple_of(lax.axis_index("dp") * width, width), width)
    slope = jnp.tanh(jnp.dot(left[...], weights[3, :, cols], preferred_element_type=F32) + biases[3:4, cols])
    deltas[...] = (adjoint[...].astype(F32) * step_size * (1.0 - slope * slope)).astype(BF16)
    return lax.dot_general(left[...], deltas[...], (((0,), (0,)), ((), ())), preferred_element_type=F32)


def own_gradient_kernel(step_size, weights, biases, left, adjoint, total, deltas):
    total[...] = gradient(step_size, weights, biases, left, adjoint, deltas, total.shape[1])


def even_kernel(step_size, rows, count, weights, biases, total, *refs):
    points, starts, adjoints = (refs[i * count : (i + 1) * count] for i in range(3))
    result, state, even, odd, adjoint, deltas = refs[3 * count :]
    here = lax.axis_index("layer")
    is_even = here % 2 == 0

    def start_from(condition, sources):
        @pl.when(condition)
        def _():
            for i, source in enumerate(sources):
                even[i * rows : (i + 1) * rows, :] = source[...]

    start_from(here == 0, points)
    start_from((here > 0) & is_even, starts)

    @pl.when(jnp.logical_not(is_even))
    def _():
        result[...] = total[...]

    @pl.when(is_even)
    def _():
        state[...] = even[...].astype(F32)
        for i, columns in enumerate(adjoints):
            adjoint[i * rows : (i + 1) * rows, :] = columns[...]
        run_layers((0, 1, 2), step_size, weights, biases, state, (even, odd))
        result[...] = total[...] + gradient(step_size, weights, biases, odd, adjoint, deltas, result.shape[1])


def odd_kernel(step_size, count, weights, biases, total, *refs):
    lefts, adjoints = refs[:count], refs[count : 2 * count]
    result, deltas = refs[2 * count :]
    result[...] = total[...]

    @pl.when(lax.axis_index("layer") % 2 == 1)
    def _():
        for left, adjoint in zip(lefts, adjoints):
            result[...] += gradient(step_size, weights, biases, left, adjoint, deltas, result.shape[1])


def single_kernel(factor, weights, biases, got, added, out):
    for cols in tiles(out.shape[1]):
        slope = layer_of(got, weights.at[0], biases[0:1, :], cols)
        out[:, cols] = got[:, cols].astype(F32) + factor * slope + added[:, cols]


def pick_kernel(chosen, new, old, out):
    here = lax.axis_index("layer")
    out[...] = jnp.where(chosen(here % 4, here // 4), new[...], old[...])


def body(inputs, guesses, weights, biases, adjoint):
    blocks = lax.axis_size("layer")
    parts = lax.axis_size("dp")
    groups = blocks // 4
    step_size = 4.0 / (4 * blocks)
    rows, depth = inputs.shape
    width = depth // parts
    layer_flops = 2 * rows * depth * depth

    def along(state, pairs):
        return lax.ppermute(state, "layer", pairs)

    def across(state, pairs, by):
        flat = [(i * parts + z, j * parts + (z + by) % parts) for i, j in pairs for z in range(parts)]
        return lax.ppermute(state, ("layer", "dp"), flat)

    def shifted(array, by):
        return lax.ppermute(array, "dp", [(i, (i + by) % parts) for i in range(parts)])

    up = [(i, i + 1) for i in range(blocks - 1)]
    up_pair = [(i, i + 1) for i in range(0, blocks, 2)]
    down_pair = [(i + 1, i) for i in range(0, blocks, 2)]
    rounded = [pltpu.VMEM((rows, depth), BF16)] * 2

    guess_sent, inputs_sent = call(round_kernel, (plain((rows, depth), BF16),) * 2, guesses[0], inputs)
    guess_prev = along(guess_sent, up)
    guess_sent, weights = lax.optimization_barrier((guess_sent, weights))
    held_weights, coarse_weight = call(
        load_kernel, (kept(weights), plain((depth, depth), BF16)), pltpu.with_memory_space_constraint(weights, pltpu.HBM),
        scratch=[pltpu.SemaphoreType.DMA((weights.shape[0] * 4 + 1,))], specs=[BULK],
    )
    guess_prev, coarse_weight = lax.optimization_barrier((guess_prev, coarse_weight))
    pair_weight = along(coarse_weight, up_pair)
    sent_adjoints = call(
        functools.partial(columns_kernel, parts), (plain((rows, width), BF16),) * parts, adjoint[0]
    )
    relaxed, relaxed_sent = call(
        functools.partial(relax_kernel, step_size, rows),
        (kept(inputs), plain((rows + EXTRA, depth), BF16)),
        held_weights, biases, inputs, guess_prev,
        scratch=rounded, flops=4 * layer_flops,
    )
    relaxed_sent, inputs_sent = lax.optimization_barrier((relaxed_sent, inputs_sent))
    relaxed_got = along(relaxed_sent, up)
    far_inputs = [across(inputs_sent, [(0, 0)], by) for by in range(1, parts)]
    start, forcing, pair_bias, ahead, forcing_sent = call(
        functools.partial(ahead_kernel, step_size, rows),
        (kept(inputs), kept(inputs), pltpu.VMEM((8, depth), F32), plain((rows, depth), BF16), plain((rows, depth), BF16)),
        held_weights, biases, inputs, relaxed_got,
        scratch=[pltpu.VMEM((rows, depth), F32)] + rounded, flops=4 * layer_flops,
    )
    pair_forcing = along(forcing_sent, up_pair)

    def two_steps(top, pairs, chosen, last=False, beside=()):
        got, *_ = lax.optimization_barrier((along(top, pairs), *beside))
        mid, *new_top = call(
            functools.partial(coarse_kernel, chosen, 4.0 * step_size),
            (kept(inputs),) if last else (kept(inputs), plain((rows, depth), BF16)),
            held_weights, biases, forcing, pair_weight, pair_bias, pair_forcing, got, top,
            scratch=rounded, flops=2 * layer_flops,
        )
        return got, mid, *new_top

    here = lax.axis_index("layer")
    slot, group = here % 4, here // 4
    last_group = groups - 1

    def single(factor, got, added):
        return call(
            functools.partial(single_kernel, factor), plain((rows, depth), F32),
            held_weights, biases, got, added, flops=layer_flops,
        )

    def finish(gots, mids):
        got_1, got_2, got_3 = gots
        mid_1, mid_2, mid_3 = mids
        held = call(held_kernel, plain((rows, depth), BF16), got_1, got_2, got_3)
        down = along(held, down_pair)
        return call(
            functools.partial(final_kernel, step_size),
            (plain((rows, depth), BF16), kept(inputs), plain((rows, depth), F32)),
            held_weights, biases, inputs, start, down, mid_2, mid_1, mid_3, forcing, relaxed,
            scratch=rounded, flops=3 * layer_flops,
        )

    top_0 = ahead
    if groups > 2:
        after = single(4.0 * step_size, along(ahead, up_pair), forcing)
        top_0 = jnp.where((slot == 1) & (group > 0), after.astype(BF16), ahead)
    got_1, mid_1, top_1 = two_steps(
        top_0, [(4 * m + 1, 4 * m + 3) for m in range(groups - 1)], lambda slot, group: (slot == 3) & (group < last_group),
        beside=far_inputs,
    )
    top_1, *sent_adjoints = lax.optimization_barrier((top_1, *sent_adjoints))
    adjoints = sent_adjoints[:1] + [shifted(sent_adjoints[by], by) for by in range(1, parts)]
    got_2, mid_2, top_2 = two_steps(
        top_1, [(4 * m - 1, 4 * m + 1) for m in range(1, groups)], lambda slot, group: (slot == 1) & (group > 0),
        beside=adjoints,
    )
    got_3, mid_3 = two_steps(
        top_2, [(4 * m + 1, 4 * m + 3) for m in range(1, groups)], lambda slot, group: (slot == 3) & (group > 0), True
    )
    top_last = top_2
    left, state, coarse_states = finish((got_1, got_2, got_3), (mid_1, mid_2, mid_3))
    if groups > 2:
        late = lambda slot, group: group > 1
        relaxed_out = call(functools.partial(pick_kernel, late), plain((rows, depth), F32), relaxed, relaxed)
        solved = coarse_states + relaxed_out
        below = along(top_1, [(4 * m - 1, 4 * m + 3) for m in range(2, groups)])
        base = solved - single(16.0 * step_size, below, jnp.zeros((rows, depth), F32))
        for m in range(2, groups):
            new = single(16.0 * step_size, along(solved.astype(BF16), [(4 * m - 1, 4 * m + 3)]), base)
            solved = jnp.where(here == 4 * m + 3, new, solved)
        new_2, new_mid_2, top_last = two_steps(
            jnp.where(slot == 3, solved.astype(BF16), top_2), [(4 * m - 1, 4 * m + 1) for m in range(2, groups)], lambda slot, group: (slot == 1) & (group > 1)
        )
        new_3, new_mid_3 = two_steps(
            top_last, [(4 * m + 1, 4 * m + 3) for m in range(2, groups)], lambda slot, group: (slot == 3) & (group > 1), True
        )
        mids = [
            call(functools.partial(pick_kernel, late), kept(inputs), new, old)
            for new, old in ((new_mid_2, mid_2), (new_mid_3, mid_3))
        ]
        gots = [jnp.where(group > 1, new, old) for new, old in ((new_2, got_2), (new_3, got_3))]
        left, state, coarse_early = finish((got_1, *gots), (mid_1, *mids))
        coarse_states = jnp.where(slot == 3, solved - relaxed_out, coarse_states)
    far = [across(top_last, [(i, i + 1) for i in range(1, blocks - 1, 2)], by) for by in range(1, parts)]
    odd_lefts = [across(left, [(i, i) for i in range(1, blocks, 2)], by) for by in range(1, parts)]
    new_states = call(
        functools.partial(last_kernel, step_size), plain((rows, depth), F32),
        held_weights, biases, left, state, flops=layer_flops,
    )
    deltas = pltpu.VMEM((rows, width), BF16)
    total = call(
        functools.partial(own_gradient_kernel, step_size), pltpu.VMEM((depth, width), F32),
        held_weights, biases, left, adjoints[0], scratch=[deltas], flops=layer_flops // 2,
    )
    others = (parts - 1) * rows
    total = call(
        functools.partial(even_kernel, step_size, rows, parts - 1), pltpu.VMEM((depth, width), F32),
        held_weights, biases, total, *far_inputs, *far, *adjoints[1:],
        scratch=[pltpu.VMEM((others, depth), F32)] + [pltpu.VMEM((others, depth), BF16)] * 2
        + [pltpu.VMEM((others, width), BF16)] * 2,
        flops=4 * (parts - 1) * layer_flops,
    )
    weight_grad = call(
        functools.partial(odd_kernel, step_size, parts - 1), plain((depth, width), F32),
        held_weights, biases, total, *odd_lefts, *adjoints[1:], scratch=[deltas], flops=2 * layer_flops,
    )
    return (new_states[None], coarse_states[None], weight_grad[None])


def solution(mesh):
    return jax.shard_map(
        body,
        mesh=mesh,
        in_specs=(
            P("dp", None),
            P("layer", "dp", None),
            P("layer", None, None),
            P("layer", None),
            P("layer", "dp", None),
        ),
        out_specs=(P("layer", "dp", None), P("layer", "dp", None), P("layer", None, "dp")),
        check_vma=False,
    )
```

```python
import functools

import jax
import jax.numpy as jnp
from jax import lax
from jax.experimental import pallas as pl
from jax.experimental.pallas import tpu as pltpu
from jax.sharding import PartitionSpec as P

BF16 = jnp.bfloat16
F32 = jnp.float32
TILE = 256
EXTRA = 16
WHOLE = pl.BlockSpec(memory_space=pltpu.VMEM)
BULK = pl.BlockSpec(memory_space=pltpu.HBM)


def call(kernel, outs, *args, scratch=(), flops=0, specs=None):
    moved = sum(a.size * a.dtype.itemsize for a in args)
    return pl.pallas_call(
        kernel,
        out_shape=outs,
        in_specs=specs or [WHOLE] * len(args),
        out_specs=jax.tree.map(lambda _: WHOLE, outs, is_leaf=lambda leaf: not isinstance(leaf, (tuple, list))),
        scratch_shapes=list(scratch),
        compiler_params=pltpu.CompilerParams(vmem_limit_bytes=8 << 20),
        cost_estimate=pl.CostEstimate(flops=flops, bytes_accessed=moved, transcendentals=0),
    )(*args)


def kept(like, dtype=None):
    return pltpu.VMEM(like.shape, dtype or like.dtype)


def plain(shape, dtype):
    return jax.ShapeDtypeStruct(shape, dtype)


def tiles(width):
    step = min(TILE, width)
    return [slice(at, at + step) for at in range(0, width, step)]


def layer_of(rounded_ref, weight_ref, bias, cols):
    product = jnp.dot(rounded_ref[...], weight_ref[:, cols], preferred_element_type=F32)
    return jnp.tanh(product + bias[:, cols])


def round_kernel(guess, sent_guess):
    sent_guess[...] = guess[...].astype(BF16)


def columns_kernel(parts, adjoint, *columns):
    width = adjoint.shape[1] // parts
    for by, target in enumerate(columns):
        index = lax.rem(lax.axis_index("dp") + by, parts)
        target[...] = adjoint[:, pl.ds(pl.multiple_of(index * width, width), width)]


def load_kernel(source, target, coarse_weight, sems):
    layers, depth = source.shape[:2]
    pieces = (sems.shape[0] - 1) // layers
    step = depth // pieces
    copies = [
        pltpu.make_async_copy(
            source.at[i, pl.ds(at * step, step)], target.at[i, pl.ds(at * step, step)], sems.at[i * pieces + at]
        )
        for i in range(layers)
        for at in range(pieces)
    ]
    for copy in copies:
        copy.start()
    for copy in copies[:pieces]:
        copy.wait()
    again = pltpu.make_async_copy(target.at[0], coarse_weight, sems.at[layers * pieces])
    again.start()
    for copy in copies[pieces:]:
        copy.wait()
    again.wait()


def run_layers(layers, step_size, weights, biases, state, rounded):
    for layer in layers:
        bias = biases[layer : layer + 1, :]
        now, later = rounded[layer % 2], rounded[(layer + 1) % 2]
        for cols in tiles(state.shape[1]):
            new = state[:, cols] + step_size * layer_of(now, weights.at[layer], bias, cols)
            state[:, cols] = new
            later[:, cols] = new.astype(BF16)


def relax_kernel(step_size, rows, weights, biases, inputs, got, relaxed, sent, sent_inputs, even, odd):
    sent_inputs[...] = inputs[...].astype(BF16)
    first = lax.axis_index("layer") == 0

    @pl.when(first)
    def _():
        relaxed[...] = inputs[...]

    @pl.when(jnp.logical_not(first))
    def _():
        relaxed[...] = got[...].astype(F32)

    even[...] = relaxed[...].astype(BF16)
    run_layers(range(4), step_size, weights, biases, relaxed, (even, odd))
    sent[:rows, :] = even[...]
    bias = biases[0:1, :]
    high = bias.astype(BF16)
    rest = bias - high.astype(F32)
    middle = rest.astype(BF16)
    low = (rest - middle.astype(F32)).astype(BF16)
    at = lax.broadcasted_iota(jnp.int32, (EXTRA, bias.shape[1]), 0)
    parts = jnp.where(at == 0, high.astype(F32), jnp.where(at == 1, middle.astype(F32), low.astype(F32)))
    sent[rows:, :] = jnp.where(at < 3, parts, 0.0).astype(BF16)


def ahead_kernel(step_size, rows, weights, biases, inputs, got, start, forcing, pair_bias, top, sent_forcing, state, even, odd):
    first = lax.axis_index("layer") == 0

    @pl.when(first)
    def _():
        start[...] = inputs[...]

    @pl.when(jnp.logical_not(first))
    def _():
        start[...] = got[:rows, :].astype(F32)

    even[...] = start[...].astype(BF16)
    bias = biases[0:1, :]
    for cols in tiles(state.shape[1]):
        slope = layer_of(even, weights.at[0], bias, cols)
        new = start[:, cols] + step_size * slope
        state[:, cols] = new
        odd[:, cols] = new.astype(BF16)
        forcing[:, cols] = start[:, cols] + (4.0 * step_size) * slope
    run_layers((1, 2, 3), step_size, weights, biases, state, (even, odd))
    top[...] = even[...]
    difference = state[...] - forcing[...]
    forcing[...] = difference
    sent_forcing[...] = difference.astype(BF16)
    tail = got[rows:, :].astype(F32)
    pair_bias[...] = jnp.broadcast_to(tail[0:1, :] + (tail[1:2, :] + tail[2:3, :]), pair_bias.shape)


def coarse_kernel(chosen, factor, weights, biases, forcing, pair_weight, pair_bias, pair_forcing, got, before, mid, *rest):
    even, odd = rest[-2:]
    here = lax.axis_index("layer")

    taken = chosen(here % 4, here // 4)

    @pl.when(jnp.logical_not(taken))
    def _():
        for top in rest[:-2]:
            top[...] = before[...]

    @pl.when(taken)
    def _():
        even[...] = got[...]
        for cols in tiles(mid.shape[1]):
            slope = layer_of(even, pair_weight, pair_bias[0:1, :], cols)
            new = got[:, cols].astype(F32) + factor * slope + pair_forcing[:, cols].astype(F32)
            mid[:, cols] = new
            odd[:, cols] = new.astype(BF16)
        bias = biases[0:1, :]
        for top in rest[:-2]:
            for cols in tiles(mid.shape[1]):
                slope = layer_of(odd, weights.at[0], bias, cols)
                top[:, cols] = (mid[:, cols] + factor * slope + forcing[:, cols]).astype(BF16)


def held_kernel(got_1, got_2, got_3, held):
    here = lax.axis_index("layer")
    low, early = here % 4 < 2, here // 4 == 0
    held[...] = jnp.where(low, got_2[...], jnp.where(early, got_1[...], got_3[...]))


def final_kernel(step_size, weights, biases, inputs, one, down, low_mid, first_mid, high_mid, forcing, relaxed, left, state, coarse, even, odd):
    here = lax.axis_index("layer")
    slot, group = here % 4, here // 4

    def start_from(condition, source):
        @pl.when(condition)
        def _():
            state[...] = source[...].astype(F32)

    start_from(here == 0, inputs)
    start_from(here == 1, one)
    start_from((here > 0) & (here % 2 == 0), down)
    start_from((slot == 1) & (group > 0), low_mid)
    start_from((slot == 3) & (group == 0), first_mid)
    start_from((slot == 3) & (group > 0), high_mid)
    even[...] = state[...].astype(BF16)
    bias = biases[0:1, :]
    for cols in tiles(state.shape[1]):
        slope = layer_of(even, weights.at[0], bias, cols)
        old = state[:, cols]
        new = old + step_size * slope
        coarse[:, cols] = old + (4.0 * step_size) * slope + forcing[:, cols] - relaxed[:, cols]
        state[:, cols] = new
        odd[:, cols] = new.astype(BF16)
    run_layers((1, 2), step_size, weights, biases, state, (even, odd))
    left[...] = odd[...]


def last_kernel(step_size, weights, biases, left, state, new_states):
    bias = biases[3:4, :]
    for cols in tiles(state.shape[1]):
        new_states[:, cols] = state[:, cols] + step_size * layer_of(left, weights.at[3], bias, cols)


def gradient(step_size, weights, biases, left, adjoint, deltas, width):
    cols = pl.ds(pl.multiple_of(lax.axis_index("dp") * width, width), width)
    slope = jnp.tanh(jnp.dot(left[...], weights[3, :, cols], preferred_element_type=F32) + biases[3:4, cols])
    deltas[...] = (adjoint[...].astype(F32) * step_size * (1.0 - slope * slope)).astype(BF16)
    return lax.dot_general(left[...], deltas[...], (((0,), (0,)), ((), ())), preferred_element_type=F32)


def own_gradient_kernel(step_size, weights, biases, left, adjoint, total, deltas):
    total[...] = gradient(step_size, weights, biases, left, adjoint, deltas, total.shape[1])


def even_kernel(step_size, rows, count, weights, biases, total, *refs):
    points, starts, adjoints = (refs[i * count : (i + 1) * count] for i in range(3))
    result, state, even, odd, adjoint, deltas = refs[3 * count :]
    here = lax.axis_index("layer")
    is_even = here % 2 == 0

    def start_from(condition, sources):
        @pl.when(condition)
        def _():
            for i, source in enumerate(sources):
                even[i * rows : (i + 1) * rows, :] = source[...]

    start_from(here == 0, points)
    start_from((here > 0) & is_even, starts)

    @pl.when(jnp.logical_not(is_even))
    def _():
        result[...] = total[...]

    @pl.when(is_even)
    def _():
        state[...] = even[...].astype(F32)
        for i, columns in enumerate(adjoints):
            adjoint[i * rows : (i + 1) * rows, :] = columns[...]
        run_layers((0, 1, 2), step_size, weights, biases, state, (even, odd))
        result[...] = total[...] + gradient(step_size, weights, biases, odd, adjoint, deltas, result.shape[1])


def odd_kernel(step_size, count, weights, biases, total, *refs):
    lefts, adjoints = refs[:count], refs[count : 2 * count]
    result, deltas = refs[2 * count :]
    result[...] = total[...]

    @pl.when(lax.axis_index("layer") % 2 == 1)
    def _():
        for left, adjoint in zip(lefts, adjoints):
            result[...] += gradient(step_size, weights, biases, left, adjoint, deltas, result.shape[1])


def single_kernel(factor, weights, biases, got, added, out):
    for cols in tiles(out.shape[1]):
        slope = layer_of(got, weights.at[0], biases[0:1, :], cols)
        out[:, cols] = got[:, cols].astype(F32) + factor * slope + added[:, cols]


def pick_kernel(chosen, new, old, out):
    here = lax.axis_index("layer")
    out[...] = jnp.where(chosen(here % 4, here // 4), new[...], old[...])


def body(inputs, guesses, weights, biases, adjoint):
    blocks = lax.axis_size("layer")
    parts = lax.axis_size("dp")
    groups = blocks // 4
    step_size = 4.0 / (4 * blocks)
    rows, depth = inputs.shape
    width = depth // parts
    layer_flops = 2 * rows * depth * depth

    def along(state, pairs):
        return lax.ppermute(state, "layer", pairs)

    def across(state, pairs, by):
        flat = [(i * parts + z, j * parts + (z + by) % parts) for i, j in pairs for z in range(parts)]
        return lax.ppermute(state, ("layer", "dp"), flat)

    def shifted(array, by):
        return lax.ppermute(array, "dp", [(i, (i + by) % parts) for i in range(parts)])

    up = [(i, i + 1) for i in range(blocks - 1)]
    up_pair = [(i, i + 1) for i in range(0, blocks, 2)]
    down_pair = [(i + 1, i) for i in range(0, blocks, 2)]
    rounded = [pltpu.VMEM((rows, depth), BF16)] * 2

    guess_sent = call(round_kernel, plain((rows, depth), BF16), guesses[0])
    guess_prev = along(guess_sent, up)
    guess_sent, weights = lax.optimization_barrier((guess_sent, weights))
    held_weights, coarse_weight = call(
        load_kernel, (kept(weights), plain((depth, depth), BF16)), pltpu.with_memory_space_constraint(weights, pltpu.HBM),
        scratch=[pltpu.SemaphoreType.DMA((weights.shape[0] * 4 + 1,))], specs=[BULK],
    )
    guess_prev, coarse_weight = lax.optimization_barrier((guess_prev, coarse_weight))
    pair_weight = along(coarse_weight, up_pair)
    sent_adjoints = call(
        functools.partial(columns_kernel, parts), (plain((rows, width), BF16),) * parts, adjoint[0]
    )
    relaxed, relaxed_sent, inputs_sent = call(
        functools.partial(relax_kernel, step_size, rows),
        (kept(inputs), plain((rows + EXTRA, depth), BF16), plain((rows, depth), BF16)),
        held_weights, biases, inputs, guess_prev,
        scratch=rounded, flops=4 * layer_flops,
    )
    relaxed_got = along(relaxed_sent, up)
    far_inputs = [across(inputs_sent, [(0, 0)], by) for by in range(1, parts)]
    start, forcing, pair_bias, ahead, forcing_sent = call(
        functools.partial(ahead_kernel, step_size, rows),
        (kept(inputs), kept(inputs), pltpu.VMEM((8, depth), F32), plain((rows, depth), BF16), plain((rows, depth), BF16)),
        held_weights, biases, inputs, relaxed_got,
        scratch=[pltpu.VMEM((rows, depth), F32)] + rounded, flops=4 * layer_flops,
    )
    pair_forcing = along(forcing_sent, up_pair)

    def two_steps(top, pairs, chosen, last=False, beside=()):
        got, *_ = lax.optimization_barrier((along(top, pairs), *beside))
        mid, *new_top = call(
            functools.partial(coarse_kernel, chosen, 4.0 * step_size),
            (kept(inputs),) if last else (kept(inputs), plain((rows, depth), BF16)),
            held_weights, biases, forcing, pair_weight, pair_bias, pair_forcing, got, top,
            scratch=rounded, flops=2 * layer_flops,
        )
        return got, mid, *new_top

    here = lax.axis_index("layer")
    slot, group = here % 4, here // 4
    last_group = groups - 1

    def single(factor, got, added):
        return call(
            functools.partial(single_kernel, factor), plain((rows, depth), F32),
            held_weights, biases, got, added, flops=layer_flops,
        )

    def finish(gots, mids):
        got_1, got_2, got_3 = gots
        mid_1, mid_2, mid_3 = mids
        held = call(held_kernel, plain((rows, depth), BF16), got_1, got_2, got_3)
        down = along(held, down_pair)
        return call(
            functools.partial(final_kernel, step_size),
            (plain((rows, depth), BF16), kept(inputs), plain((rows, depth), F32)),
            held_weights, biases, inputs, start, down, mid_2, mid_1, mid_3, forcing, relaxed,
            scratch=rounded, flops=3 * layer_flops,
        )

    top_0 = ahead
    if groups > 2:
        after = single(4.0 * step_size, along(ahead, up_pair), forcing)
        top_0 = jnp.where((slot == 1) & (group > 0), after.astype(BF16), ahead)
    got_1, mid_1, top_1 = two_steps(
        top_0, [(4 * m + 1, 4 * m + 3) for m in range(groups - 1)], lambda slot, group: (slot == 3) & (group < last_group),
        beside=far_inputs,
    )
    top_1, *sent_adjoints = lax.optimization_barrier((top_1, *sent_adjoints))
    adjoints = sent_adjoints[:1] + [shifted(sent_adjoints[by], by) for by in range(1, parts)]
    got_2, mid_2, top_2 = two_steps(
        top_1, [(4 * m - 1, 4 * m + 1) for m in range(1, groups)], lambda slot, group: (slot == 1) & (group > 0),
        beside=adjoints,
    )
    got_3, mid_3 = two_steps(
        top_2, [(4 * m + 1, 4 * m + 3) for m in range(1, groups)], lambda slot, group: (slot == 3) & (group > 0), True
    )
    top_last = top_2
    left, state, coarse_states = finish((got_1, got_2, got_3), (mid_1, mid_2, mid_3))
    if groups > 2:
        late = lambda slot, group: group > 1
        relaxed_out = call(functools.partial(pick_kernel, late), plain((rows, depth), F32), relaxed, relaxed)
        solved = coarse_states + relaxed_out
        below = along(top_1, [(4 * m - 1, 4 * m + 3) for m in range(2, groups)])
        base = solved - single(16.0 * step_size, below, jnp.zeros((rows, depth), F32))
        for m in range(2, groups):
            new = single(16.0 * step_size, along(solved.astype(BF16), [(4 * m - 1, 4 * m + 3)]), base)
            solved = jnp.where(here == 4 * m + 3, new, solved)
        new_2, new_mid_2, top_last = two_steps(
            jnp.where(slot == 3, solved.astype(BF16), top_2), [(4 * m - 1, 4 * m + 1) for m in range(2, groups)], lambda slot, group: (slot == 1) & (group > 1)
        )
        new_3, new_mid_3 = two_steps(
            top_last, [(4 * m + 1, 4 * m + 3) for m in range(2, groups)], lambda slot, group: (slot == 3) & (group > 1), True
        )
        mids = [
            call(functools.partial(pick_kernel, late), kept(inputs), new, old)
            for new, old in ((new_mid_2, mid_2), (new_mid_3, mid_3))
        ]
        gots = [jnp.where(group > 1, new, old) for new, old in ((new_2, got_2), (new_3, got_3))]
        left, state, coarse_early = finish((got_1, *gots), (mid_1, *mids))
        coarse_states = jnp.where(slot == 3, solved - relaxed_out, coarse_states)
    far = [across(top_last, [(i, i + 1) for i in range(1, blocks - 1, 2)], by) for by in range(1, parts)]
    odd_lefts = [across(left, [(i, i) for i in range(1, blocks, 2)], by) for by in range(1, parts)]
    new_states = call(
        functools.partial(last_kernel, step_size), plain((rows, depth), F32),
        held_weights, biases, left, state, flops=layer_flops,
    )
    deltas = pltpu.VMEM((rows, width), BF16)
    total = call(
        functools.partial(own_gradient_kernel, step_size), pltpu.VMEM((depth, width), F32),
        held_weights, biases, left, adjoints[0], scratch=[deltas], flops=layer_flops // 2,
    )
    others = (parts - 1) * rows
    total = call(
        functools.partial(even_kernel, step_size, rows, parts - 1), pltpu.VMEM((depth, width), F32),
        held_weights, biases, total, *far_inputs, *far, *adjoints[1:],
        scratch=[pltpu.VMEM((others, depth), F32)] + [pltpu.VMEM((others, depth), BF16)] * 2
        + [pltpu.VMEM((others, width), BF16)] * 2,
        flops=4 * (parts - 1) * layer_flops,
    )
    weight_grad = call(
        functools.partial(odd_kernel, step_size, parts - 1), plain((depth, width), F32),
        held_weights, biases, total, *odd_lefts, *adjoints[1:], scratch=[deltas], flops=2 * layer_flops,
    )
    return (new_states[None], coarse_states[None], weight_grad[None])


def solution(mesh):
    return jax.shard_map(
        body,
        mesh=mesh,
        in_specs=(
            P("dp", None),
            P("layer", "dp", None),
            P("layer", None, None),
            P("layer", None),
            P("layer", "dp", None),
        ),
        out_specs=(P("layer", "dp", None), P("layer", "dp", None), P("layer", None, "dp")),
        check_vma=False,
    )
```

```python
import functools

import jax
import jax.numpy as jnp
from jax import lax
from jax.experimental import pallas as pl
from jax.experimental.pallas import tpu as pltpu
from jax.sharding import PartitionSpec as P

BF16 = jnp.bfloat16
F32 = jnp.float32
TILE = 256
EXTRA = 16
WHOLE = pl.BlockSpec(memory_space=pltpu.VMEM)
BULK = pl.BlockSpec(memory_space=pltpu.HBM)


def call(kernel, outs, *args, scratch=(), flops=0, specs=None):
    moved = sum(a.size * a.dtype.itemsize for a in args)
    return pl.pallas_call(
        kernel,
        out_shape=outs,
        in_specs=specs or [WHOLE] * len(args),
        out_specs=jax.tree.map(lambda _: WHOLE, outs, is_leaf=lambda leaf: not isinstance(leaf, (tuple, list))),
        scratch_shapes=list(scratch),
        compiler_params=pltpu.CompilerParams(vmem_limit_bytes=8 << 20),
        cost_estimate=pl.CostEstimate(flops=flops, bytes_accessed=moved, transcendentals=0),
    )(*args)


def kept(like, dtype=None):
    return pltpu.VMEM(like.shape, dtype or like.dtype)


def plain(shape, dtype):
    return jax.ShapeDtypeStruct(shape, dtype)


def tiles(width):
    step = min(TILE, width)
    return [slice(at, at + step) for at in range(0, width, step)]


def layer_of(rounded_ref, weight_ref, bias, cols):
    product = jnp.dot(rounded_ref[...], weight_ref[:, cols], preferred_element_type=F32)
    return jnp.tanh(product + bias[:, cols])


def round_kernel(guess, sent_guess):
    sent_guess[...] = guess[...].astype(BF16)


def columns_kernel(parts, adjoint, *columns):
    width = adjoint.shape[1] // parts
    for by, target in enumerate(columns):
        index = lax.rem(lax.axis_index("dp") + by, parts)
        target[...] = adjoint[:, pl.ds(pl.multiple_of(index * width, width), width)]


def load_kernel(source, target, coarse_weight, sems):
    layers, depth = source.shape[:2]
    pieces = (sems.shape[0] - 1) // layers
    step = depth // pieces
    copies = [
        pltpu.make_async_copy(
            source.at[i, pl.ds(at * step, step)], target.at[i, pl.ds(at * step, step)], sems.at[i * pieces + at]
        )
        for i in range(layers)
        for at in range(pieces)
    ]
    for copy in copies:
        copy.start()
    for copy in copies[:pieces]:
        copy.wait()
    again = pltpu.make_async_copy(target.at[0], coarse_weight, sems.at[layers * pieces])
    again.start()
    for copy in copies[pieces:]:
        copy.wait()
    again.wait()


def run_layers(layers, step_size, weights, biases, state, rounded):
    for layer in layers:
        bias = biases[layer : layer + 1, :]
        now, later = rounded[layer % 2], rounded[(layer + 1) % 2]
        for cols in tiles(state.shape[1]):
            new = state[:, cols] + step_size * layer_of(now, weights.at[layer], bias, cols)
            state[:, cols] = new
            later[:, cols] = new.astype(BF16)


def relax_kernel(step_size, rows, weights, biases, inputs, got, relaxed, sent, sent_inputs, even, odd):
    sent_inputs[...] = inputs[...].astype(BF16)
    first = lax.axis_index("layer") == 0

    @pl.when(first)
    def _():
        relaxed[...] = inputs[...]

    @pl.when(jnp.logical_not(first))
    def _():
        relaxed[...] = got[...].astype(F32)

    even[...] = relaxed[...].astype(BF16)
    run_layers(range(4), step_size, weights, biases, relaxed, (even, odd))
    sent[:rows, :] = even[...]
    bias = biases[0:1, :]
    high = bias.astype(BF16)
    rest = bias - high.astype(F32)
    middle = rest.astype(BF16)
    low = (rest - middle.astype(F32)).astype(BF16)
    at = lax.broadcasted_iota(jnp.int32, (EXTRA, bias.shape[1]), 0)
    parts = jnp.where(at == 0, high.astype(F32), jnp.where(at == 1, middle.astype(F32), low.astype(F32)))
    sent[rows:, :] = jnp.where(at < 3, parts, 0.0).astype(BF16)


def ahead_kernel(step_size, rows, weights, biases, inputs, got, start, forcing, pair_bias, top, sent_forcing, state, even, odd):
    first = lax.axis_index("layer") == 0

    @pl.when(first)
    def _():
        start[...] = inputs[...]

    @pl.when(jnp.logical_not(first))
    def _():
        start[...] = got[:rows, :].astype(F32)

    even[...] = start[...].astype(BF16)
    bias = biases[0:1, :]
    for cols in tiles(state.shape[1]):
        slope = layer_of(even, weights.at[0], bias, cols)
        new = start[:, cols] + step_size * slope
        state[:, cols] = new
        odd[:, cols] = new.astype(BF16)
        forcing[:, cols] = start[:, cols] + (4.0 * step_size) * slope
    run_layers((1, 2, 3), step_size, weights, biases, state, (even, odd))
    top[...] = even[...]
    difference = state[...] - forcing[...]
    forcing[...] = difference
    sent_forcing[...] = difference.astype(BF16)
    tail = got[rows:, :].astype(F32)
    pair_bias[...] = jnp.broadcast_to(tail[0:1, :] + (tail[1:2, :] + tail[2:3, :]), pair_bias.shape)


def coarse_kernel(chosen, factor, weights, biases, forcing, pair_weight, pair_bias, pair_forcing, got, before, mid, *rest):
    even, odd = rest[-2:]
    here = lax.axis_index("layer")

    taken = chosen(here % 4, here // 4)

    @pl.when(jnp.logical_not(taken))
    def _():
        for top in rest[:-2]:
            top[...] = before[...]

    @pl.when(taken)
    def _():
        even[...] = got[...]
        for cols in tiles(mid.shape[1]):
            slope = layer_of(even, pair_weight, pair_bias[0:1, :], cols)
            new = got[:, cols].astype(F32) + factor * slope + pair_forcing[:, cols].astype(F32)
            mid[:, cols] = new
            odd[:, cols] = new.astype(BF16)
        bias = biases[0:1, :]
        for top in rest[:-2]:
            for cols in tiles(mid.shape[1]):
                slope = layer_of(odd, weights.at[0], bias, cols)
                top[:, cols] = (mid[:, cols] + factor * slope + forcing[:, cols]).astype(BF16)


def held_kernel(got_1, got_2, got_3, after, held):
    here = lax.axis_index("layer")
    low, early = here % 4 < 2, here // 4 == 0
    held[...] = jnp.where(low, got_2[...], jnp.where(early, got_1[...], got_3[...]))


def final_kernel(step_size, weights, biases, inputs, one, down, low_mid, first_mid, high_mid, forcing, relaxed, left, state, coarse, even, odd):
    here = lax.axis_index("layer")
    slot, group = here % 4, here // 4

    def start_from(condition, source):
        @pl.when(condition)
        def _():
            state[...] = source[...].astype(F32)

    start_from(here == 0, inputs)
    start_from(here == 1, one)
    start_from((here > 0) & (here % 2 == 0), down)
    start_from((slot == 1) & (group > 0), low_mid)
    start_from((slot == 3) & (group == 0), first_mid)
    start_from((slot == 3) & (group > 0), high_mid)
    even[...] = state[...].astype(BF16)
    bias = biases[0:1, :]
    for cols in tiles(state.shape[1]):
        slope = layer_of(even, weights.at[0], bias, cols)
        old = state[:, cols]
        new = old + step_size * slope
        coarse[:, cols] = old + (4.0 * step_size) * slope + forcing[:, cols] - relaxed[:, cols]
        state[:, cols] = new
        odd[:, cols] = new.astype(BF16)
    run_layers((1, 2), step_size, weights, biases, state, (even, odd))
    left[...] = odd[...]


def last_kernel(step_size, weights, biases, left, state, new_states):
    bias = biases[3:4, :]
    for cols in tiles(state.shape[1]):
        new_states[:, cols] = state[:, cols] + step_size * layer_of(left, weights.at[3], bias, cols)


def gradient(step_size, weights, biases, left, adjoint, deltas, width):
    cols = pl.ds(pl.multiple_of(lax.axis_index("dp") * width, width), width)
    slope = jnp.tanh(jnp.dot(left[...], weights[3, :, cols], preferred_element_type=F32) + biases[3:4, cols])
    deltas[...] = (adjoint[...].astype(F32) * step_size * (1.0 - slope * slope)).astype(BF16)
    return lax.dot_general(left[...], deltas[...], (((0,), (0,)), ((), ())), preferred_element_type=F32)


def own_gradient_kernel(step_size, weights, biases, left, adjoint, total, deltas):
    total[...] = gradient(step_size, weights, biases, left, adjoint, deltas, total.shape[1])


def even_kernel(step_size, rows, count, weights, biases, total, *refs):
    points, starts, adjoints = (refs[i * count : (i + 1) * count] for i in range(3))
    result, state, even, odd, adjoint, deltas = refs[3 * count :]
    here = lax.axis_index("layer")
    is_even = here % 2 == 0

    def start_from(condition, sources):
        @pl.when(condition)
        def _():
            for i, source in enumerate(sources):
                even[i * rows : (i + 1) * rows, :] = source[...]

    start_from(here == 0, points)
    start_from((here > 0) & is_even, starts)

    @pl.when(jnp.logical_not(is_even))
    def _():
        result[...] = total[...]

    @pl.when(is_even)
    def _():
        state[...] = even[...].astype(F32)
        for i, columns in enumerate(adjoints):
            adjoint[i * rows : (i + 1) * rows, :] = columns[...]
        run_layers((0, 1, 2), step_size, weights, biases, state, (even, odd))
        result[...] = total[...] + gradient(step_size, weights, biases, odd, adjoint, deltas, result.shape[1])


def odd_kernel(step_size, count, weights, biases, total, *refs):
    lefts, adjoints = refs[:count], refs[count : 2 * count]
    result, deltas = refs[2 * count :]
    result[...] = total[...]

    @pl.when(lax.axis_index("layer") % 2 == 1)
    def _():
        for left, adjoint in zip(lefts, adjoints):
            result[...] += gradient(step_size, weights, biases, left, adjoint, deltas, result.shape[1])


def single_kernel(factor, weights, biases, got, added, out):
    for cols in tiles(out.shape[1]):
        slope = layer_of(got, weights.at[0], biases[0:1, :], cols)
        out[:, cols] = got[:, cols].astype(F32) + factor * slope + added[:, cols]


def pick_kernel(chosen, new, old, out):
    here = lax.axis_index("layer")
    out[...] = jnp.where(chosen(here % 4, here // 4), new[...], old[...])


def body(inputs, guesses, weights, biases, adjoint):
    blocks = lax.axis_size("layer")
    parts = lax.axis_size("dp")
    groups = blocks // 4
    step_size = 4.0 / (4 * blocks)
    rows, depth = inputs.shape
    width = depth // parts
    layer_flops = 2 * rows * depth * depth

    def along(state, pairs):
        return lax.ppermute(state, "layer", pairs)

    def across(state, pairs, by):
        flat = [(i * parts + z, j * parts + (z + by) % parts) for i, j in pairs for z in range(parts)]
        return lax.ppermute(state, ("layer", "dp"), flat)

    def shifted(array, by):
        return lax.ppermute(array, "dp", [(i, (i + by) % parts) for i in range(parts)])

    up = [(i, i + 1) for i in range(blocks - 1)]
    up_pair = [(i, i + 1) for i in range(0, blocks, 2)]
    down_pair = [(i + 1, i) for i in range(2, blocks, 2)]
    rounded = [pltpu.VMEM((rows, depth), BF16)] * 2

    guess_sent = call(round_kernel, plain((rows, depth), BF16), guesses[0])
    guess_prev = along(guess_sent, up)
    guess_sent, weights = lax.optimization_barrier((guess_sent, weights))
    held_weights, coarse_weight = call(
        load_kernel, (kept(weights), plain((depth, depth), BF16)), pltpu.with_memory_space_constraint(weights, pltpu.HBM),
        scratch=[pltpu.SemaphoreType.DMA((weights.shape[0] * 4 + 1,))], specs=[BULK],
    )
    guess_prev, coarse_weight = lax.optimization_barrier((guess_prev, coarse_weight))
    pair_weight = along(coarse_weight, up_pair)
    sent_adjoints = call(
        functools.partial(columns_kernel, parts), (plain((rows, width), BF16),) * parts, adjoint[0]
    )
    relaxed, relaxed_sent, inputs_sent = call(
        functools.partial(relax_kernel, step_size, rows),
        (kept(inputs), plain((rows + EXTRA, depth), BF16), plain((rows, depth), BF16)),
        held_weights, biases, inputs, guess_prev,
        scratch=rounded, flops=4 * layer_flops,
    )
    relaxed_got = along(relaxed_sent, up)
    far_inputs = [across(inputs_sent, [(0, 0)], by) for by in range(1, parts)]
    start, forcing, pair_bias, ahead, forcing_sent = call(
        functools.partial(ahead_kernel, step_size, rows),
        (kept(inputs), kept(inputs), pltpu.VMEM((8, depth), F32), plain((rows, depth), BF16), plain((rows, depth), BF16)),
        held_weights, biases, inputs, relaxed_got,
        scratch=[pltpu.VMEM((rows, depth), F32)] + rounded, flops=4 * layer_flops,
    )
    pair_forcing = along(forcing_sent, up_pair)

    def two_steps(top, pairs, chosen, last=False, beside=()):
        got, *_ = lax.optimization_barrier((along(top, pairs), *beside))
        mid, *new_top = call(
            functools.partial(coarse_kernel, chosen, 4.0 * step_size),
            (kept(inputs),) if last else (kept(inputs), plain((rows, depth), BF16)),
            held_weights, biases, forcing, pair_weight, pair_bias, pair_forcing, got, top,
            scratch=rounded, flops=2 * layer_flops,
        )
        return got, mid, *new_top

    here = lax.axis_index("layer")
    slot, group = here % 4, here // 4
    last_group = groups - 1

    def single(factor, got, added):
        return call(
            functools.partial(single_kernel, factor), plain((rows, depth), F32),
            held_weights, biases, got, added, flops=layer_flops,
        )

    def finish(gots, mids):
        got_1, got_2, got_3 = gots
        mid_1, mid_2, mid_3 = mids
        held = call(held_kernel, plain((rows, depth), BF16), got_1, got_2, got_3, mid_3)
        down = along(held, down_pair)
        return down, *call(
            functools.partial(final_kernel, step_size),
            (plain((rows, depth), BF16), kept(inputs), plain((rows, depth), F32)),
            held_weights, biases, inputs, start, down, mid_2, mid_1, mid_3, forcing, relaxed,
            scratch=rounded, flops=3 * layer_flops,
        )

    top_0 = ahead
    if groups > 2:
        after = single(4.0 * step_size, along(ahead, up_pair), forcing)
        top_0 = jnp.where((slot == 1) & (group > 0), after.astype(BF16), ahead)
    got_1, mid_1, top_1 = two_steps(
        top_0, [(4 * m + 1, 4 * m + 3) for m in range(groups - 1)], lambda slot, group: (slot == 3) & (group < last_group),
        beside=far_inputs,
    )
    top_1, *sent_adjoints = lax.optimization_barrier((top_1, *sent_adjoints))
    adjoints = sent_adjoints[:1] + [shifted(sent_adjoints[by], by) for by in range(1, parts)]
    got_2, mid_2, top_2 = two_steps(
        top_1, [(4 * m - 1, 4 * m + 1) for m in range(1, groups)], lambda slot, group: (slot == 1) & (group > 0),
        beside=adjoints,
    )
    got_3, mid_3 = two_steps(
        top_2, [(4 * m + 1, 4 * m + 3) for m in range(1, groups)], lambda slot, group: (slot == 3) & (group > 0), True
    )
    top_last = top_2
    down, left, state, coarse_states = finish((got_1, got_2, got_3), (mid_1, mid_2, mid_3))
    if groups > 2:
        late = lambda slot, group: group > 1
        relaxed_out = call(functools.partial(pick_kernel, late), plain((rows, depth), F32), relaxed, relaxed)
        solved = coarse_states + relaxed_out
        below = along(top_1, [(4 * m - 1, 4 * m + 3) for m in range(2, groups)])
        base = solved - single(16.0 * step_size, below, jnp.zeros((rows, depth), F32))
        for m in range(2, groups):
            new = single(16.0 * step_size, along(solved.astype(BF16), [(4 * m - 1, 4 * m + 3)]), base)
            solved = jnp.where(here == 4 * m + 3, new, solved)
        new_2, new_mid_2, top_last = two_steps(
            jnp.where(slot == 3, solved.astype(BF16), top_2), [(4 * m - 1, 4 * m + 1) for m in range(2, groups)], lambda slot, group: (slot == 1) & (group > 1)
        )
        new_3, new_mid_3 = two_steps(
            top_last, [(4 * m + 1, 4 * m + 3) for m in range(2, groups)], lambda slot, group: (slot == 3) & (group > 1), True
        )
        mids = [
            call(functools.partial(pick_kernel, late), kept(inputs), new, old)
            for new, old in ((new_mid_2, mid_2), (new_mid_3, mid_3))
        ]
        gots = [jnp.where(group > 1, new, old) for new, old in ((new_2, got_2), (new_3, got_3))]
        down, left, state, coarse_early = finish((got_1, *gots), (mid_1, *mids))
        coarse_states = jnp.where(slot == 3, solved - relaxed_out, coarse_states)
    onward = [(i, i + 1) for i in range(1, blocks - 1, 2)]
    last_even = [(blocks - 2, blocks - 2)]
    newest = call(
        functools.partial(pick_kernel, lambda slot, group: slot % 2 == 0), plain((rows, depth), BF16), down, top_last
    )
    far = [
        across(newest, onward[:-1] + last_even, by) if 2 * by == parts else across(top_last, onward, by)
        for by in range(1, parts)
    ]
    odd_lefts = [across(left, [(i, i) for i in range(1, blocks, 2)], by) for by in range(1, parts)]
    new_states = call(
        functools.partial(last_kernel, step_size), plain((rows, depth), F32),
        held_weights, biases, left, state, flops=layer_flops,
    )
    deltas = pltpu.VMEM((rows, width), BF16)
    total = call(
        functools.partial(own_gradient_kernel, step_size), pltpu.VMEM((depth, width), F32),
        held_weights, biases, left, adjoints[0], scratch=[deltas], flops=layer_flops // 2,
    )
    others = (parts - 1) * rows
    total = call(
        functools.partial(even_kernel, step_size, rows, parts - 1), pltpu.VMEM((depth, width), F32),
        held_weights, biases, total, *far_inputs, *far, *adjoints[1:],
        scratch=[pltpu.VMEM((others, depth), F32)] + [pltpu.VMEM((others, depth), BF16)] * 2
        + [pltpu.VMEM((others, width), BF16)] * 2,
        flops=4 * (parts - 1) * layer_flops,
    )
    for at, out in ((slice(0, parts - 2), pltpu.VMEM((depth, width), F32)), (slice(parts - 2, parts), plain((depth, width), F32))):
        batch = odd_lefts[at]
        total = call(
            functools.partial(odd_kernel, step_size, len(batch)), out,
            held_weights, biases, total, *batch, *adjoints[1:][at], scratch=[deltas], flops=len(batch) * layer_flops // 2,
        )
    weight_grad = total
    return (new_states[None], coarse_states[None], weight_grad[None])


def solution(mesh):
    return jax.shard_map(
        body,
        mesh=mesh,
        in_specs=(
            P("dp", None),
            P("layer", "dp", None),
            P("layer", None, None),
            P("layer", None),
            P("layer", "dp", None),
        ),
        out_specs=(P("layer", "dp", None), P("layer", "dp", None), P("layer", None, "dp")),
        check_vma=False,
    )
```
